32 devices in a mesh: ens: 4 (over y, x), lat: 8 (over z, core).
Axes of the slice: x: 2, y: 2, z: 4, core: 2. Of those that a mesh axis runs over, the one named last changes fastest.
Arguments:
- prediction_array: float32 [16, 16, 64, 1440], P('ens', None, 'lat'), may hold values from -6 to 6
- verifying_analysis: float32 [16, 64, 1440], P('ens', 'lat'), may hold values from -6 to 6
- variable_penalty_factor: float32 [16], replicated, may hold values from 0.25 to 4
Outputs:
- field_grad: float32 [16, 16, 64, 1440], P('ens', None, 'lat')
The draws below stay inside these ranges and needn't reach their ends.
All inputs are finite; a program needn't handle non-finite values.
Results may differ from the reference program's by a relative error of at most 0.00002.
Values sent between devices are 32-bit elements; how exact they have to be, the bound alone decides.
A program may use at most 64 MiB of HBM per device.

```python
import math
import jax
import jax.numpy as jnp
from jax import lax

ENSEMBLE_SIZE = 16
VARIABLE_NUMBER = 16
MERIDIAN_NUMBER = 1440
COARSE = 3
PARALLEL_NUMBER = 64


def block_levels(rng, extent, cuts, low, top_value):
    loudness, own = 1.0, jax.random.fold_in(rng, 6)
    for axis_at, blocks in cuts:
        heights = jnp.exp(jax.random.uniform(jax.random.fold_in(own, axis_at), (blocks,), jnp.float32, low / len(cuts), top_value / len(cuts)))
        loudness = loudness * jnp.repeat(heights, extent[axis_at] // blocks).reshape([-1 if axis == axis_at else 1 for axis in range(len(extent))])
    return loudness


def normal_values(own_key, dims, spread, limit, cuts=(), held_as=jnp.bfloat16):
    array = jax.random.normal(own_key, dims, jnp.float32) * spread
    if len(cuts) > 0:
        array = block_levels(own_key, dims, cuts, -0.22, 0.18) * array
    return jnp.clip(array, min=-limit, max=limit).astype(held_as)


def setup_inputs(seed: int = 0) -> dict:
    splits = jax.random.split(jax.random.key(seed), 4)
    prediction_array = normal_values(splits[0], (ENSEMBLE_SIZE, VARIABLE_NUMBER, PARALLEL_NUMBER, MERIDIAN_NUMBER), 1.0, 6.0, ((0, 4), (2, 8)), jnp.float32)
    verifying_analysis = normal_values(splits[1], (VARIABLE_NUMBER, PARALLEL_NUMBER, MERIDIAN_NUMBER), 1.0, 6.0, ((0, 4), (1, 8)), jnp.float32)
    variable_penalty_factor = jnp.clip(jnp.exp(jax.random.uniform(splits[2], (VARIABLE_NUMBER,), jnp.float32, math.log(0.25), math.log(4.0))), 0.25, 4.0)
    return dict(prediction_array=prediction_array, verifying_analysis=verifying_analysis, variable_penalty_factor=variable_penalty_factor)


def normal_kernel_smoother(field):
    widths = [(0, 0)] * (field.ndim - 2) + [(1, 1), (0, 0)]
    padded = jnp.pad(field, widths)
    along = 0.25 * padded[..., :-2, :] + 0.5 * padded[..., 1:-1, :] + 0.25 * padded[..., 2:, :]
    return 0.25 * jnp.roll(along, 1, -1) + 0.5 * along + 0.25 * jnp.roll(along, -1, -1)

def slope(differ):
    return differ * lax.rsqrt(differ * differ + 0.01)

def couple_derivative(smooth_fc, smooth_obs, penalty_factor):
    count = smooth_fc.shape[0]

    def single(member):
        return lax.optimization_barrier(jnp.sum(slope(member[None] - smooth_fc), axis=0))
    pulls = lax.map(single, smooth_fc)
    return penalty_factor * (slope(smooth_fc - smooth_obs[None]) - 0.95 / (count - 1) * pulls)

def reference(prediction_array, verifying_analysis, variable_penalty_factor):
    sharp_prediction = normal_kernel_smoother(prediction_array)
    smooth_prediction = sharp_prediction
    sharp_analysis = normal_kernel_smoother(verifying_analysis)
    coarse_obs = sharp_analysis
    for repeat in range(COARSE - 1):
        smooth_prediction = normal_kernel_smoother(smooth_prediction)
        coarse_obs = normal_kernel_smoother(coarse_obs)
    rows_all = jnp.arange(PARALLEL_NUMBER).astype(jnp.float32)
    degrees = 0.25 * (rows_all - (PARALLEL_NUMBER - 1) / 2.0)
    lat_weight = jnp.cos(jnp.deg2rad(degrees))
    penalty_factor = variable_penalty_factor[:, None, None] * lat_weight[None, :, None]
    sharp_derivative = couple_derivative(sharp_prediction, sharp_analysis, penalty_factor)
    grad_coarse = couple_derivative(smooth_prediction, coarse_obs, penalty_factor)
    level = grad_coarse
    for repeat in range(COARSE - 1):
        level = normal_kernel_smoother(level)
    return normal_kernel_smoother(sharp_derivative + level)
```

```python
import functools

import jax
import jax.numpy as jnp
import numpy as np
from jax import lax
from jax.experimental import pallas as pl
from jax.experimental.pallas import tpu as pltpu
from jax.sharding import PartitionSpec as P

COARSE = 3
LANES = 128
MESH = pl.DeviceIdType.MESH


def round_up(value, unit):
    return -(-value // unit) * unit


def band_matrices(fields, rows):
    half = rows // 2
    pairs = fields // 2
    out = np.zeros((4, 2 * fields * rows, 2 * fields * rows), np.float32)
    window = 2 * rows
    band = 0.5 * np.eye(window) + 0.25 * np.eye(window, k=1) + 0.25 * np.eye(window, k=-1)
    places = np.arange(window) - half
    for variant in range(4):
        keep = np.ones(window)
        if variant & 1:
            keep[places < 0] = 0.0
        if variant & 2:
            keep[places >= rows] = 0.0
        step = keep[:, None] * band * keep[None, :]
        scales = (step, np.linalg.matrix_power(step, COARSE))
        for scale, matrix in enumerate(scales):
            matrix = matrix[half : half + rows]
            for field in range(fields):
                at = (scale * fields + field) * rows
                out[variant, at : at + rows, field * rows : (field + 1) * rows] = matrix[:, half : half + rows]
                tile, part = field % pairs, field // pairs
                low = (fields + tile) * rows + part * half
                out[variant, at : at + rows, low : low + half] = matrix[:, :half]
                high = (fields + pairs + tile) * rows + part * half
                out[variant, at : at + rows, high : high + half] = matrix[:, half + rows :]
    return out


def split_dot(matrix, values):
    first = values.astype(jnp.bfloat16)
    rest = values - first.astype(jnp.float32)
    second = rest.astype(jnp.bfloat16)
    third = (rest - second.astype(jnp.float32)).astype(jnp.bfloat16)
    total = jnp.dot(matrix, third, preferred_element_type=jnp.float32)
    total = total + jnp.dot(matrix, second, preferred_element_type=jnp.float32)
    return total + jnp.dot(matrix, first, preferred_element_type=jnp.float32)


def wrapped(tiles, width):
    whole = width // LANES
    rest = width - whole * LANES
    last = tiles[:, whole * LANES :]
    lane = lax.broadcasted_iota(jnp.int32, last.shape, 1)
    ahead = pltpu.roll(tiles[:, :LANES], rest, 1)
    behind = pltpu.roll(last, LANES - rest, 1)
    last = jnp.where(lane < rest, last, jnp.where(lane < (LANES + rest) // 2, ahead, behind))
    return jnp.concatenate([tiles[:, : whole * LANES], last], axis=1)


def lon_pass(tiles):
    size = tiles.shape[1]
    return 0.25 * (pltpu.roll(tiles, 1, 1) + pltpu.roll(tiles, size - 1, 1)) + 0.5 * tiles


def lon_blur(ref, count, width):
    def step(field, carry):
        ref[field] = lon_pass(wrapped(ref[field], width))
        coarse = wrapped(ref[count + field], width)
        for _ in range(COARSE):
            coarse = lon_pass(coarse)
        ref[count + field] = coarse
        return carry

    lax.fori_loop(0, count, step, 0)


def slope(differ):
    return differ * lax.rsqrt(differ * differ + 0.01)


def kernel(
    dims,
    in_ref, obs_ref, factor_ref, weight_ref, band_ref, back_ref, obs_band_ref,
    main_ref, rest_ref,
    staged, fields, rests, rest_out, halo_out, obs_fields, obs_halo, obs_sm, smooth, result, result_rest,
    edge_out, edge_in,
    f_send, f_recv, fr_send, fr_recv, own_sem, stage_sem,
    h_send, h_recv, oh_send, oh_recv, e_send, e_recv,
    b_send, b_recv, br_send, br_recv, bown_sem, brown_sem,
):
    ens_n, lat_n, local, members, group, rows, width = dims
    half = rows // 2
    pairs = members // 2
    full = width // LANES * LANES
    rest = width - full
    padded = full + LANES
    me = lax.axis_index("ens")
    lat = lax.axis_index("lat")
    has_low = lat > 0
    has_high = lat < lat_n - 1
    variant = (lat == 0).astype(jnp.int32) + 2 * (lat == lat_n - 1).astype(jnp.int32)

    def peer(shift):
        return lax.rem(me + shift, ens_n)

    barrier = pltpu.get_barrier_semaphore()
    for shift in range(1, ens_n):
        pl.semaphore_signal(barrier, inc=1, device_id={"ens": peer(shift)}, device_id_type=MESH)

    @pl.when(has_low)
    def _():
        pl.semaphore_signal(barrier, inc=1, device_id={"lat": lat - 1}, device_id_type=MESH)

    @pl.when(has_high)
    def _():
        pl.semaphore_signal(barrier, inc=1, device_id={"lat": lat + 1}, device_id_type=MESH)

    stage = pltpu.make_async_copy(in_ref, staged, stage_sem)
    stage.start()

    def zero_edges(low):
        at = members if low else members + pairs
        side = 0 if low else 1

        def clear(k, carry):
            def tile(p, inner):
                fields[k, at + p] = jnp.zeros((rows, padded), jnp.float32)
                edge_in[k, side, p] = jnp.zeros((rows, padded), jnp.float32)
                return inner

            lax.fori_loop(0, pairs, tile, 0)
            return carry

        lax.fori_loop(0, group, clear, 0)
        obs_at = group if low else group + group // 2
        for p in range(group // 2):
            obs_fields[obs_at + p] = jnp.zeros((rows, padded), jnp.float32)

    @pl.when(jnp.logical_not(has_low))
    def _():
        zero_edges(True)

    @pl.when(jnp.logical_not(has_high))
    def _():
        zero_edges(False)

    pl.semaphore_wait(barrier, ens_n - 1 + has_low.astype(jnp.int32) + has_high.astype(jnp.int32))

    def f_main(k, shift):
        target = peer(shift)
        return pltpu.make_async_remote_copy(
            src_ref=in_ref.at[:, target * group + k, :, pl.ds(0, full)],
            dst_ref=fields.at[k, pl.ds(me * local, local), :, pl.ds(0, full)],
            send_sem=f_send.at[k, shift], recv_sem=f_recv.at[k, shift],
            device_id={"ens": target}, device_id_type=MESH,
        )

    def f_rest(k, shift):
        target = peer(shift)
        return pltpu.make_async_remote_copy(
            src_ref=rest_out.at[k, target], dst_ref=rests.at[k, me],
            send_sem=fr_send.at[k, shift], recv_sem=fr_recv.at[k, shift],
            device_id={"ens": target}, device_id_type=MESH,
        )

    def f_own(k):
        return pltpu.make_async_copy(
            in_ref.at[:, me * group + k, :, pl.ds(0, full)],
            fields.at[k, pl.ds(me * local, local), :, pl.ds(0, full)],
            own_sem.at[k],
        )

    def start_main(k):
        for shift in range(1, ens_n):
            f_main(k, shift).start()
        f_own(k).start()

    lane = lax.broadcasted_iota(jnp.int32, (rows, LANES), 1)

    def packed(tiles):
        total = tiles[0]
        for m in range(1, local):
            total = jnp.where(lane < m * rest, total, pltpu.roll(tiles[m], m * rest, 1))
        return total

    def start_rest(k):
        for target in range(ens_n):
            tile = packed([
                jnp.concatenate(
                    [staged[m, target * group + k, :, pl.ds(full, rest)],
                     jnp.zeros((rows, LANES - rest), jnp.float32)], axis=1)
                for m in range(local)
            ])
            rest_out[k, target] = tile
        rests[k, me] = rest_out[k, me]
        for shift in range(1, ens_n):
            f_rest(k, shift).start()

    ahead = min(2, group)
    start_main(0)
    stage.wait()
    start_rest(0)
    for k in range(1, ahead):
        start_main(k)
        start_rest(k)

    upper = lax.broadcasted_iota(jnp.int32, (rows, padded), 0) < half

    def turn(tile):
        return pltpu.roll(tile, half, 0)

    def neighbour_copies(source, targets, send, recv):
        return (
            pltpu.make_async_remote_copy(
                src_ref=source[0], dst_ref=targets[1], send_sem=send.at[0], recv_sem=recv.at[1],
                device_id={"lat": lat - 1}, device_id_type=MESH,
            ),
            pltpu.make_async_remote_copy(
                src_ref=source[1], dst_ref=targets[0], send_sem=send.at[1], recv_sem=recv.at[0],
                device_id={"lat": lat + 1}, device_id_type=MESH,
            ),
        )

    def start_both(copies):
        @pl.when(has_low)
        def _():
            copies[0].start()

        @pl.when(has_high)
        def _():
            copies[1].start()

    def recv_both(copies):
        @pl.when(has_low)
        def _():
            copies[1].wait_recv()

        @pl.when(has_high)
        def _():
            copies[0].wait_recv()

    def sent_both(copies):
        @pl.when(has_low)
        def _():
            copies[0].wait_send()

        @pl.when(has_high)
        def _():
            copies[1].wait_send()

    def halo_copies(k):
        return neighbour_copies(
            (halo_out.at[k, 0], halo_out.at[k, 1]),
            (fields.at[k, pl.ds(members, pairs)], fields.at[k, pl.ds(members + pairs, pairs)]),
            h_send.at[k], h_recv.at[k],
        )

    def edge_copies(k):
        return neighbour_copies(
            (edge_out.at[k, 0], edge_out.at[k, 1]), (edge_in.at[k, 0], edge_in.at[k, 1]),
            e_send.at[k], e_recv.at[k],
        )

    couples = group // 2
    obs_copies = neighbour_copies(
        (obs_halo.at[0], obs_halo.at[1]),
        (obs_fields.at[pl.ds(group, couples)], obs_fields.at[pl.ds(group + couples, couples)]),
        oh_send, oh_recv,
    )
    for c in range(group):
        obs_fields[c, :, pl.ds(full, LANES)] = jnp.zeros((rows, LANES), jnp.float32)
        obs_fields[c, :, pl.ds(0, width)] = obs_ref[c]
    for p in range(couples):
        one, two = obs_fields[p], obs_fields[p + couples]
        obs_halo[0, p] = jnp.where(upper, one, turn(two))
        obs_halo[1, p] = jnp.where(upper, turn(one), two)
    start_both(obs_copies)
    recv_both(obs_copies)
    values = obs_fields[...].reshape(2 * group * rows, padded)
    obs_sm[...] = split_dot(obs_band_ref[variant], values).reshape(2 * group, rows, padded)
    lon_blur(obs_sm, group, width)

    def take_fields(k):
        for shift in range(1, ens_n):
            f_main(k, shift).wait_recv()
            f_rest(k, shift).wait_recv()
        f_own(k).wait()

        def unpack(source, carry):
            tile = rests[k, source]
            for m in range(local):
                fields[k, source * local + m, :, pl.ds(full, LANES)] = (
                    pltpu.roll(tile, LANES - m * rest, 1) if m else tile
                )
            return carry

        lax.fori_loop(0, ens_n, unpack, 0)

        def pack_halo(p, carry):
            one, two = fields[k, p], fields[k, p + pairs]
            halo_out[k, 0, p] = jnp.where(upper, one, turn(two))
            halo_out[k, 1, p] = jnp.where(upper, turn(one), two)
            return carry

        lax.fori_loop(0, pairs, pack_halo, 0)
        start_both(halo_copies(k))

        @pl.when(k + ahead < group)
        def _():
            start_main(k + ahead)
            start_rest(k + ahead)

    block = 2 * LANES if padded % (2 * LANES) == 0 else LANES
    total_rows = 2 * members * rows

    def compute(k):
        recv_both(halo_copies(k))

        def smooth_block(b, carry):
            at = pl.ds(pl.multiple_of(b * block, block), block)
            values = fields[k, :, :, at].reshape(total_rows, block)
            smooth[:, :, at] = split_dot(band_ref[variant], values).reshape(2 * members, rows, block)
            return carry

        lax.fori_loop(0, padded // block, smooth_block, 0)
        lon_blur(smooth, members, width)
        weight = factor_ref[me * group + k] * weight_ref[lat]
        pull = 0.95 / (members - 1)
        tiles = padded // LANES

        def couple(i, carry):
            scale, t = i // tiles, i % tiles
            at = pl.ds(pl.multiple_of(t * LANES, LANES), LANES)
            base = scale * members
            held = [smooth[base + m, :, at] for m in range(members)]
            sums = [None] * members
            for m in range(members):
                for other in range(m):
                    force = slope(held[m] - held[other])
                    sums[m] = force if sums[m] is None else sums[m] + force
                    sums[other] = -force if sums[other] is None else sums[other] - force
            analysis = obs_sm[scale * group + k, :, at]
            for m in range(members):
                smooth[base + m, :, at] = weight * (slope(held[m] - analysis) - pull * sums[m])
            return carry

        lax.fori_loop(0, 2 * tiles, couple, 0)
        lon_blur(smooth, members, width)

        def back_block(b, carry):
            at = pl.ds(pl.multiple_of(b * block, block), block)
            values = smooth[:, :, at].reshape(total_rows, block)
            out = split_dot(back_ref[variant], values).reshape(2 * members, rows, block)
            result[k, :, :, at] = out[:members]
            edge_out[k, 0, :, :, at] = out[members : members + pairs]
            edge_out[k, 1, :, :, at] = out[members + pairs :]
            return carry

        lax.fori_loop(0, padded // block, back_block, 0)
        start_both(edge_copies(k))

    def b_main(k, shift):
        target = peer(shift)
        return pltpu.make_async_remote_copy(
            src_ref=result.at[k, pl.ds(target * local, local), :, pl.ds(0, full)],
            dst_ref=main_ref.at[:, me * group + k],
            send_sem=b_send.at[k, shift], recv_sem=b_recv.at[k, shift],
            device_id={"ens": target}, device_id_type=MESH,
        )

    def b_rest(k, shift):
        target = peer(shift)
        return pltpu.make_async_remote_copy(
            src_ref=result_rest.at[k, target], dst_ref=rest_ref.at[me * group + k],
            send_sem=br_send.at[k, shift], recv_sem=br_recv.at[k, shift],
            device_id={"ens": target}, device_id_type=MESH,
        )

    def b_own(k):
        return (
            pltpu.make_async_copy(
                result.at[k, pl.ds(me * local, local), :, pl.ds(0, full)],
                main_ref.at[:, me * group + k], bown_sem.at[k],
            ),
            pltpu.make_async_copy(
                result_rest.at[k, me], rest_ref.at[me * group + k], brown_sem.at[k]
            ),
        )

    def finish(k):
        recv_both(edge_copies(k))

        def add(p, carry):
            low, high = edge_in[k, 0, p], edge_in[k, 1, p]
            result[k, p] = result[k, p] + jnp.where(upper, low, turn(high))
            result[k, p + pairs] = result[k, p + pairs] + jnp.where(upper, turn(low), high)
            return carry

        lax.fori_loop(0, pairs, add, 0)

        def pack(target, carry):
            result_rest[k, target] = packed(
                [result[k, target * local + m, :, pl.ds(full, LANES)] for m in range(local)]
            )
            return carry

        lax.fori_loop(0, ens_n, pack, 0)
        for shift in range(1, ens_n):
            b_main(k, shift).start()
            b_rest(k, shift).start()
        for copy in b_own(k):
            copy.start()

    take_fields(0)

    def turn_of(k, carry):
        @pl.when(k + 1 < group)
        def _():
            take_fields(k + 1)

        compute(k)

        @pl.when(k > 0)
        def _():
            finish(k - 1)

        return carry

    lax.fori_loop(0, group, turn_of, 0)
    finish(group - 1)

    sent_both(obs_copies)

    def drain(k, carry):
        for shift in range(1, ens_n):
            f_main(k, shift).wait_send()
            f_rest(k, shift).wait_send()
            b_main(k, shift).wait()
            b_rest(k, shift).wait()
        for copy in b_own(k):
            copy.wait()
        sent_both(halo_copies(k))
        sent_both(edge_copies(k))
        return carry

    lax.fori_loop(0, group, drain, 0)


def unpack_kernel(rest, main_ref, rest_ref, out_ref):
    local, _, _, full = main_ref.shape
    tile = rest_ref[...]
    for m in range(local):
        out_ref[m, :, :, pl.ds(0, full)] = main_ref[m]
        out_ref[m, :, :, pl.ds(full, rest)] = tile[:, :, m * rest : (m + 1) * rest]


def body(prediction_array, verifying_analysis, variable_penalty_factor):
    local, channels, rows, width = prediction_array.shape
    group = verifying_analysis.shape[0]
    ens_n, lat_n = lax.axis_size("ens"), lax.axis_size("lat")
    members = local * ens_n
    pairs = members // 2
    full = width // LANES * LANES
    rest = width - full
    padded = full + LANES
    assert rows % 8 == 0 and rows // 2 >= COARSE and local * rest <= LANES and channels == group * ens_n
    assert members % 2 == 0 and group % 2 == 0 and LANES - rest >= 4 * COARSE

    bands = band_matrices(members, rows)
    band = jnp.asarray(bands, jnp.bfloat16)
    back = jnp.asarray(np.ascontiguousarray(bands.transpose(0, 2, 1)), jnp.bfloat16)
    obs_band = jnp.asarray(band_matrices(group, rows), jnp.bfloat16)
    ids = np.arange(lat_n * rows).astype(np.float32)
    degrees = np.float32(0.25) * (ids - np.float32((lat_n * rows - 1) / 2.0))
    weights = np.cos(degrees * np.float32(np.pi / 180.0)).astype(np.float32).reshape(lat_n, rows, 1)
    weights = jnp.asarray(np.broadcast_to(weights, (lat_n, rows, LANES)))

    dims = (ens_n, lat_n, local, members, group, rows, width)
    vmem = pl.BlockSpec(memory_space=pltpu.VMEM)
    hbm = pl.BlockSpec(memory_space=pl.ANY)
    f32 = jnp.float32
    dma = pltpu.SemaphoreType.DMA
    cells = group * padded * rows
    main, rests = pl.pallas_call(
        functools.partial(kernel, dims),
        out_shape=(
            jax.ShapeDtypeStruct((local, channels, rows, full), f32),
            jax.ShapeDtypeStruct((channels, rows, LANES), f32),
        ),
        in_specs=[hbm, vmem, pl.BlockSpec(memory_space=pltpu.SMEM), vmem, vmem, vmem, vmem],
        out_specs=(hbm, hbm),
        scratch_shapes=[
            pltpu.VMEM((local, channels, rows, width), f32),
            pltpu.VMEM((group, members + 2 * pairs, rows, padded), f32),
            pltpu.VMEM((group, ens_n, rows, LANES), f32),
            pltpu.VMEM((group, ens_n, rows, LANES), f32),
            pltpu.VMEM((group, 2, pairs, rows, padded), f32),
            pltpu.VMEM((2 * group, rows, padded), f32),
            pltpu.VMEM((2, group // 2, rows, padded), f32),
            pltpu.VMEM((2 * group, rows, padded), f32),
            pltpu.VMEM((2 * members, rows, padded), f32),
            pltpu.VMEM((group, members, rows, padded), f32),
            pltpu.VMEM((group, ens_n, rows, LANES), f32),
            pltpu.VMEM((group, 2, pairs, rows, padded), f32),
            pltpu.VMEM((group, 2, pairs, rows, padded), f32),
            dma((group, ens_n)), dma((group, ens_n)), dma((group, ens_n)), dma((group, ens_n)),
            dma((group,)), dma,
            dma((group, 2)), dma((group, 2)), dma((2,)), dma((2,)), dma((group, 2)), dma((group, 2)),
            dma((group, ens_n)), dma((group, ens_n)), dma((group, ens_n)), dma((group, ens_n)),
            dma((group,)), dma((group,)),
        ],
        compiler_params=pltpu.CompilerParams(
            collective_id=0, has_side_effects=True, vmem_limit_bytes=48 * 1024 * 1024
        ),
        cost_estimate=pl.CostEstimate(
            flops=cells * members * members * 6, bytes_accessed=cells * members * 8,
            transcendentals=cells * members * members,
        ),
    )(prediction_array, verifying_analysis, variable_penalty_factor, weights, band, back, obs_band)

    part = group
    return pl.pallas_call(
        functools.partial(unpack_kernel, rest),
        grid=(channels // part,),
        out_shape=jax.ShapeDtypeStruct((local, channels, rows, width), f32),
        in_specs=[
            pl.BlockSpec((local, part, rows, full), lambda i: (0, i, 0, 0)),
            pl.BlockSpec((part, rows, LANES), lambda i: (i, 0, 0)),
        ],
        out_specs=pl.BlockSpec((local, part, rows, width), lambda i: (0, i, 0, 0)),
    )(main, rests)


def solution(mesh):
    placed = (P("ens", None, "lat", None), P("ens", "lat", None), P())
    return jax.shard_map(
        body, mesh=mesh, in_specs=placed, out_specs=P("ens", None, "lat", None), check_vma=False
    )
```

```python
import functools
import math

import jax
import jax.numpy as jnp
import numpy as np
from jax import lax
from jax.experimental import pallas as pl
from jax.experimental.pallas import tpu as pltpu
from jax.sharding import PartitionSpec as P

COARSE = 3
LANES = 128
MESH = pl.DeviceIdType.MESH


def round_up(value, unit):
    return -(-value // unit) * unit


def band_matrices(fields, rows):
    half = rows // 2
    pairs = fields // 2
    out = np.zeros((4, 2 * fields * rows, 2 * fields * rows), np.float32)
    window = 2 * rows
    band = 0.5 * np.eye(window) + 0.25 * np.eye(window, k=1) + 0.25 * np.eye(window, k=-1)
    places = np.arange(window) - half
    for variant in range(4):
        keep = np.ones(window)
        if variant & 1:
            keep[places < 0] = 0.0
        if variant & 2:
            keep[places >= rows] = 0.0
        step = keep[:, None] * band * keep[None, :]
        scales = (step, np.linalg.matrix_power(step, COARSE))
        for scale, matrix in enumerate(scales):
            matrix = matrix[half : half + rows]
            for field in range(fields):
                at = (scale * fields + field) * rows
                out[variant, at : at + rows, field * rows : (field + 1) * rows] = matrix[:, half : half + rows]
                tile, part = field % pairs, field // pairs
                low = (fields + tile) * rows + part * half
                out[variant, at : at + rows, low : low + half] = matrix[:, :half]
                high = (fields + pairs + tile) * rows + part * half
                out[variant, at : at + rows, high : high + half] = matrix[:, half + rows :]
    return out


def split_dot(matrix, values, parts):
    pieces = []
    for _ in range(parts):
        piece = values.astype(jnp.bfloat16)
        pieces.append(piece)
        values = values - piece.astype(jnp.float32)
    return jnp.dot(matrix, jnp.concatenate(pieces, axis=0), preferred_element_type=jnp.float32)


def wrapped(tiles, width):
    whole = width // LANES
    rest = width - whole * LANES
    last = tiles[:, whole * LANES :]
    lane = lax.broadcasted_iota(jnp.int32, last.shape, 1)
    ahead = pltpu.roll(tiles[:, :LANES], rest, 1)
    behind = pltpu.roll(last, LANES - rest, 1)
    last = jnp.where(lane < rest, last, jnp.where(lane < (LANES + rest) // 2, ahead, behind))
    return jnp.concatenate([tiles[:, : whole * LANES], last], axis=1)


def lon_pass(tiles, passes):
    size = tiles.shape[1]
    total = math.comb(2 * passes, passes) / 4.0**passes * tiles
    for far in range(1, passes + 1):
        both = pltpu.roll(tiles, far, 1) + pltpu.roll(tiles, size - far, 1)
        total = total + math.comb(2 * passes, passes + far) / 4.0**passes * both
    return total


def lon_blur(ref, count, width):
    def step(field, carry):
        ref[field] = lon_pass(wrapped(ref[field], width), 1)
        ref[count + field] = lon_pass(wrapped(ref[count + field], width), COARSE)
        return carry

    lax.fori_loop(0, count, step, 0, unroll=2)


def slope(differ):
    return differ * lax.rsqrt(differ * differ + 0.01)


def kernel(
    dims,
    in_ref, obs_hbm, factor_ref, weight_hbm, band_hbm, back_hbm, obs_band_hbm,
    out_ref,
    main_ref, rest_ref, obs_ref, weight_ref, band_ref, back_ref, obs_band_ref,
    staged, fields, rests, rest_out, halo_out, obs_fields, obs_halo, obs_sm, smooth, result, result_rest,
    edge_out, edge_in,
    f_send, f_recv, fr_send, fr_recv, own_sem, stage_sem,
    h_send, h_recv, oh_send, oh_recv, e_send, e_recv,
    b_send, b_recv, br_send, br_recv, bown_sem, load_sem, out_sem,
):
    ens_n, lat_n, local, members, group, rows, width = dims
    half = rows // 2
    pairs = members // 2
    full = width // LANES * LANES
    rest = width - full
    padded = full + LANES
    me = lax.axis_index("ens")
    lat = lax.axis_index("lat")
    has_low = lat > 0
    has_high = lat < lat_n - 1
    variant = (lat == 0).astype(jnp.int32) + 2 * (lat == lat_n - 1).astype(jnp.int32)

    def peer(shift):
        return lax.rem(me + shift, ens_n)

    barrier = pltpu.get_barrier_semaphore()
    for shift in range(1, ens_n):
        pl.semaphore_signal(barrier, inc=1, device_id={"ens": peer(shift)}, device_id_type=MESH)

    @pl.when(has_low)
    def _():
        pl.semaphore_signal(barrier, inc=1, device_id={"lat": lat - 1}, device_id_type=MESH)

    @pl.when(has_high)
    def _():
        pl.semaphore_signal(barrier, inc=1, device_id={"lat": lat + 1}, device_id_type=MESH)

    stage = pltpu.make_async_copy(in_ref, staged, stage_sem)
    stage.start()
    loads = [
        pltpu.make_async_copy(source, target, load_sem.at[i])
        for i, (source, target) in enumerate((
            (obs_hbm, obs_ref),
            (weight_hbm.at[lat], weight_ref),
            (band_hbm.at[variant], band_ref),
            (back_hbm.at[variant], back_ref),
            (obs_band_hbm.at[variant], obs_band_ref),
        ))
    ]
    for load in loads:
        load.start()

    def zero_edges(low):
        at = members if low else members + pairs
        side = 0 if low else 1

        def clear(k, carry):
            def tile(p, inner):
                fields[k, at + p] = jnp.zeros((rows, padded), jnp.float32)
                edge_in[k, side, p] = jnp.zeros((rows, padded), jnp.float32)
                return inner

            lax.fori_loop(0, pairs, tile, 0)
            return carry

        lax.fori_loop(0, group, clear, 0)
        obs_at = group if low else group + group // 2
        for p in range(group // 2):
            obs_fields[obs_at + p] = jnp.zeros((rows, padded), jnp.float32)

    @pl.when(jnp.logical_not(has_low))
    def _():
        zero_edges(True)

    @pl.when(jnp.logical_not(has_high))
    def _():
        zero_edges(False)

    pl.semaphore_wait(barrier, ens_n - 1 + has_low.astype(jnp.int32) + has_high.astype(jnp.int32))

    def f_main(k, shift):
        target = peer(shift)
        return pltpu.make_async_remote_copy(
            src_ref=in_ref.at[:, target * group + k, :, pl.ds(0, full)],
            dst_ref=fields.at[k, pl.ds(me * local, local), :, pl.ds(0, full)],
            send_sem=f_send.at[k, shift], recv_sem=f_recv.at[k, shift],
            device_id={"ens": target}, device_id_type=MESH,
        )

    def f_rest(k, shift):
        target = peer(shift)
        return pltpu.make_async_remote_copy(
            src_ref=rest_out.at[k, target], dst_ref=rests.at[k, me],
            send_sem=fr_send.at[k, shift], recv_sem=fr_recv.at[k, shift],
            device_id={"ens": target}, device_id_type=MESH,
        )

    def f_own(k):
        return pltpu.make_async_copy(
            in_ref.at[:, me * group + k, :, pl.ds(0, full)],
            fields.at[k, pl.ds(me * local, local), :, pl.ds(0, full)],
            own_sem.at[k],
        )

    def start_main(k):
        for shift in range(1, ens_n):
            f_main(k, shift).start()
        f_own(k).start()

    lane = lax.broadcasted_iota(jnp.int32, (rows, LANES), 1)

    def packed(tiles):
        total = tiles[0]
        for m in range(1, local):
            total = jnp.where(lane < m * rest, total, pltpu.roll(tiles[m], m * rest, 1))
        return total

    def start_rest(k):
        for target in range(ens_n):
            tile = packed([
                jnp.concatenate(
                    [staged[m, target * group + k, :, pl.ds(full, rest)],
                     jnp.zeros((rows, LANES - rest), jnp.float32)], axis=1)
                for m in range(local)
            ])
            rest_out[k, target] = tile
        rests[k, me] = rest_out[k, me]
        for shift in range(1, ens_n):
            f_rest(k, shift).start()

    ahead = min(2, group)
    start_main(0)
    stage.wait()
    start_rest(0)
    upper = lax.broadcasted_iota(jnp.int32, (rows, padded), 0) < half

    def turn(tile):
        return pltpu.roll(tile, half, 0)

    def neighbour_copies(source, targets, send, recv):
        return (
            pltpu.make_async_remote_copy(
                src_ref=source[0], dst_ref=targets[1], send_sem=send.at[0], recv_sem=recv.at[1],
                device_id={"lat": lat - 1}, device_id_type=MESH,
            ),
            pltpu.make_async_remote_copy(
                src_ref=source[1], dst_ref=targets[0], send_sem=send.at[1], recv_sem=recv.at[0],
                device_id={"lat": lat + 1}, device_id_type=MESH,
            ),
        )

    def start_both(copies):
        @pl.when(has_low)
        def _():
            copies[0].start()

        @pl.when(has_high)
        def _():
            copies[1].start()

    def recv_both(copies):
        @pl.when(has_low)
        def _():
            copies[1].wait_recv()

        @pl.when(has_high)
        def _():
            copies[0].wait_recv()

    def sent_both(copies):
        @pl.when(has_low)
        def _():
            copies[0].wait_send()

        @pl.when(has_high)
        def _():
            copies[1].wait_send()

    def halo_copies(k):
        return neighbour_copies(
            (halo_out.at[k, 0], halo_out.at[k, 1]),
            (fields.at[k, pl.ds(members, pairs)], fields.at[k, pl.ds(members + pairs, pairs)]),
            h_send.at[k], h_recv.at[k],
        )

    def edge_copies(k):
        return neighbour_copies(
            (edge_out.at[k, 0], edge_out.at[k, 1]), (edge_in.at[k, 0], edge_in.at[k, 1]),
            e_send.at[k], e_recv.at[k],
        )

    for load in loads:
        load.wait()
    couples = group // 2
    obs_copies = neighbour_copies(
        (obs_halo.at[0], obs_halo.at[1]),
        (obs_fields.at[pl.ds(group, couples)], obs_fields.at[pl.ds(group + couples, couples)]),
        oh_send, oh_recv,
    )
    for c in range(group):
        obs_fields[c, :, pl.ds(full, LANES)] = jnp.zeros((rows, LANES), jnp.float32)
        obs_fields[c, :, pl.ds(0, width)] = obs_ref[c]
    for p in range(couples):
        one, two = obs_fields[p], obs_fields[p + couples]
        obs_halo[0, p] = jnp.where(upper, one, turn(two))
        obs_halo[1, p] = jnp.where(upper, turn(one), two)
    start_both(obs_copies)
    for k in range(1, ahead):
        start_main(k)
        start_rest(k)
    recv_both(obs_copies)
    values = obs_fields[...].reshape(2 * group * rows, padded)
    obs_sm[...] = split_dot(obs_band_ref[...], values, 3).reshape(2 * group, rows, padded)
    lon_blur(obs_sm, group, width)

    def take_fields(k):
        for shift in range(1, ens_n):
            f_main(k, shift).wait_recv()
            f_rest(k, shift).wait_recv()
        f_own(k).wait()

        def unpack(source, carry):
            tile = rests[k, source]
            for m in range(local):
                fields[k, source * local + m, :, pl.ds(full, LANES)] = (
                    pltpu.roll(tile, LANES - m * rest, 1) if m else tile
                )
            return carry

        lax.fori_loop(0, ens_n, unpack, 0)

        def pack_halo(p, carry):
            one, two = fields[k, p], fields[k, p + pairs]
            halo_out[k, 0, p] = jnp.where(upper, one, turn(two))
            halo_out[k, 1, p] = jnp.where(upper, turn(one), two)
            return carry

        lax.fori_loop(0, pairs, pack_halo, 0)
        start_both(halo_copies(k))

        @pl.when(k + ahead < group)
        def _():
            start_main(k + ahead)
            start_rest(k + ahead)

    block = 2 * LANES if padded % (2 * LANES) == 0 else LANES
    total_rows = 2 * members * rows

    def forward(k):
        recv_both(halo_copies(k))

        def smooth_block(b, carry):
            at = pl.ds(pl.multiple_of(b * block, block), block)
            values = fields[k, :, :, at].reshape(total_rows, block)
            smooth[:, :, at] = split_dot(band_ref[...], values, 3).reshape(2 * members, rows, block)
            return carry

        lax.fori_loop(0, padded // block, smooth_block, 0, unroll=3 if padded // block % 3 == 0 else 1)
        lon_blur(smooth, members, width)
        weight = factor_ref[me * group + k] * weight_ref[...]
        pull = 0.95 / (members - 1)
        tiles = padded // LANES

        def couple(i, carry):
            scale, t = i // tiles, i % tiles
            at = pl.ds(pl.multiple_of(t * LANES, LANES), LANES)
            base = scale * members
            held = [smooth[base + m, :, at] for m in range(members)]
            sums = [None] * members
            for m in range(members):
                for other in range(m):
                    force = slope(held[m] - held[other])
                    sums[m] = force if sums[m] is None else sums[m] + force
                    sums[other] = -force if sums[other] is None else sums[other] - force
            analysis = obs_sm[scale * group + k, :, at]
            for m in range(members):
                smooth[base + m, :, at] = weight * (slope(held[m] - analysis) - pull * sums[m])
            return carry

        lax.fori_loop(0, 2 * tiles, couple, 0)

    def backward(k):
        lon_blur(smooth, members, width)

        def back_block(b, carry):
            at = pl.ds(pl.multiple_of(b * block, block), block)
            values = smooth[:, :, at].reshape(total_rows, block)
            out = split_dot(back_ref[...], values, 2).reshape(2 * members, rows, block)
            result[k, :, :, at] = out[:members]
            edge_out[k, 0, :, :, at] = out[members : members + pairs]
            edge_out[k, 1, :, :, at] = out[members + pairs :]
            return carry

        lax.fori_loop(0, padded // block, back_block, 0, unroll=3 if padded // block % 3 == 0 else 1)
        start_both(edge_copies(k))

    def b_main(k, shift):
        target = peer(shift)
        return pltpu.make_async_remote_copy(
            src_ref=result.at[k, pl.ds(target * local, local), :, pl.ds(0, full)],
            dst_ref=main_ref.at[:, me * group + k, :, pl.ds(0, full)],
            send_sem=b_send.at[k, shift], recv_sem=b_recv.at[k, shift],
            device_id={"ens": target}, device_id_type=MESH,
        )

    def b_rest(k, shift):
        target = peer(shift)
        return pltpu.make_async_remote_copy(
            src_ref=result_rest.at[k, target], dst_ref=rest_ref.at[me * group + k],
            send_sem=br_send.at[k, shift], recv_sem=br_recv.at[k, shift],
            device_id={"ens": target}, device_id_type=MESH,
        )

    def b_own(k):
        return pltpu.make_async_copy(
            result.at[k, pl.ds(me * local, local), :, pl.ds(0, full)],
            main_ref.at[:, me * group + k, :, pl.ds(0, full)], bown_sem.at[k],
        )

    def write(k, source):
        channel = source * group + k
        return pltpu.make_async_copy(
            main_ref.at[:, channel], out_ref.at[:, channel], out_sem.at[k, source]
        )

    def finish(k):
        recv_both(edge_copies(k))

        def add(p, carry):
            low, high = edge_in[k, 0, p], edge_in[k, 1, p]
            result[k, p] = result[k, p] + jnp.where(upper, low, turn(high))
            result[k, p + pairs] = result[k, p + pairs] + jnp.where(upper, turn(low), high)
            return carry

        lax.fori_loop(0, pairs, add, 0)

        def pack(target, carry):
            result_rest[k, target] = packed(
                [result[k, target * local + m, :, pl.ds(full, LANES)] for m in range(local)]
            )
            return carry

        lax.fori_loop(0, ens_n, pack, 0)
        for shift in range(1, ens_n):
            b_main(k, shift).start()
            b_rest(k, shift).start()
        b_own(k).start()
        rest_ref[me * group + k] = result_rest[k, me]

    take_fields(0)

    def turn_of(k, carry):
        forward(k)

        @pl.when(k + 1 < group)
        def _():
            take_fields(k + 1)

        backward(k)

        @pl.when(k > 0)
        def _():
            finish(k - 1)

        return carry

    lax.fori_loop(0, group, turn_of, 0)
    finish(group - 1)

    sent_both(obs_copies)

    def drain(k, carry):
        for shift in range(1, ens_n):
            b_main(k, shift).wait_recv()
            b_rest(k, shift).wait_recv()
        b_own(k).wait()

        def unpack(source, inner):
            channel = source * group + k
            tile = rest_ref[channel]
            for m in range(local):
                main_ref[m, channel, :, pl.ds(full, rest)] = tile[:, m * rest : (m + 1) * rest]
            write(k, source).start()
            return inner

        lax.fori_loop(0, ens_n, unpack, 0)
        for shift in range(1, ens_n):
            f_main(k, shift).wait_send()
            f_rest(k, shift).wait_send()
            b_main(k, shift).wait_send()
            b_rest(k, shift).wait_send()
        sent_both(halo_copies(k))
        sent_both(edge_copies(k))
        return carry

    lax.fori_loop(0, group, drain, 0)

    def close(k, carry):
        for source in range(ens_n):
            write(k, source).wait()
        return carry

    lax.fori_loop(0, group, close, 0)


def body(prediction_array, verifying_analysis, variable_penalty_factor):
    local, channels, rows, width = prediction_array.shape
    group = verifying_analysis.shape[0]
    ens_n, lat_n = lax.axis_size("ens"), lax.axis_size("lat")
    members = local * ens_n
    pairs = members // 2
    full = width // LANES * LANES
    rest = width - full
    padded = full + LANES
    assert rows % 8 == 0 and rows // 2 >= COARSE and local * rest <= LANES and channels == group * ens_n
    assert members % 2 == 0 and group % 2 == 0 and LANES - rest >= 4 * COARSE

    bands = band_matrices(members, rows)
    band = jnp.asarray(np.concatenate([bands] * 3, axis=2), jnp.bfloat16)
    back = jnp.asarray(np.concatenate([bands.transpose(0, 2, 1)] * 2, axis=2), jnp.bfloat16)
    obs_bands = band_matrices(group, rows)
    obs_band = jnp.asarray(np.concatenate([obs_bands] * 3, axis=2), jnp.bfloat16)
    ids = np.arange(lat_n * rows).astype(np.float32)
    degrees = np.float32(0.25) * (ids - np.float32((lat_n * rows - 1) / 2.0))
    weights = np.cos(degrees * np.float32(np.pi / 180.0)).astype(np.float32).reshape(lat_n, rows, 1)
    weights = jnp.asarray(np.broadcast_to(weights, (lat_n, rows, LANES)))

    dims = (ens_n, lat_n, local, members, group, rows, width)
    hbm = pl.BlockSpec(memory_space=pl.ANY)
    f32 = jnp.float32
    dma = pltpu.SemaphoreType.DMA
    cells = group * padded * rows
    return pl.pallas_call(
        functools.partial(kernel, dims),
        out_shape=jax.ShapeDtypeStruct((local, channels, rows, width), f32),
        in_specs=[hbm, hbm, pl.BlockSpec(memory_space=pltpu.SMEM), hbm, hbm, hbm, hbm],
        out_specs=hbm,
        scratch_shapes=[
            pltpu.VMEM((local, channels, rows, width), f32),
            pltpu.VMEM((channels, rows, LANES), f32),
            pltpu.VMEM(verifying_analysis.shape, f32),
            pltpu.VMEM(weights.shape[1:], f32),
            pltpu.VMEM(band.shape[1:], jnp.bfloat16),
            pltpu.VMEM(back.shape[1:], jnp.bfloat16),
            pltpu.VMEM(obs_band.shape[1:], jnp.bfloat16),
            pltpu.VMEM((local, channels, rows, width), f32),
            pltpu.VMEM((group, members + 2 * pairs, rows, padded), f32),
            pltpu.VMEM((group, ens_n, rows, LANES), f32),
            pltpu.VMEM((group, ens_n, rows, LANES), f32),
            pltpu.VMEM((group, 2, pairs, rows, padded), f32),
            pltpu.VMEM((2 * group, rows, padded), f32),
            pltpu.VMEM((2, group // 2, rows, padded), f32),
            pltpu.VMEM((2 * group, rows, padded), f32),
            pltpu.VMEM((2 * members, rows, padded), f32),
            pltpu.VMEM((group, members, rows, padded), f32),
            pltpu.VMEM((group, ens_n, rows, LANES), f32),
            pltpu.VMEM((group, 2, pairs, rows, padded), f32),
            pltpu.VMEM((group, 2, pairs, rows, padded), f32),
            dma((group, ens_n)), dma((group, ens_n)), dma((group, ens_n)), dma((group, ens_n)),
            dma((group,)), dma,
            dma((group, 2)), dma((group, 2)), dma((2,)), dma((2,)), dma((group, 2)), dma((group, 2)),
            dma((group, ens_n)), dma((group, ens_n)), dma((group, ens_n)), dma((group, ens_n)),
            dma((group,)), dma((5,)), dma((group, ens_n)),
        ],
        compiler_params=pltpu.CompilerParams(
            collective_id=0, has_side_effects=True, vmem_limit_bytes=48 * 1024 * 1024
        ),
        cost_estimate=pl.CostEstimate(
            flops=cells * members * members * 6, bytes_accessed=cells * members * 8,
            transcendentals=cells * members * members,
        ),
    )(prediction_array, verifying_analysis, variable_penalty_factor, weights, band, back, obs_band)


def solution(mesh):
    placed = (P("ens", None, "lat", None), P("ens", "lat", None), P())
    return jax.shard_map(
        body, mesh=mesh, in_specs=placed, out_specs=P("ens", None, "lat", None), check_vma=False
    )
```

```python
import functools
import math

import jax
import jax.numpy as jnp
import numpy as np
from jax import lax
from jax.experimental import pallas as pl
from jax.experimental.pallas import tpu as pltpu
from jax.sharding import PartitionSpec as P

COARSE = 3
LANES = 128
MESH = pl.DeviceIdType.MESH


def round_up(value, unit):
    return -(-value // unit) * unit


def band_matrices(fields, rows):
    half = rows // 2
    pairs = fields // 2
    out = np.zeros((4, 2 * fields * rows, 2 * fields * rows), np.float32)
    window = 2 * rows
    band = 0.5 * np.eye(window) + 0.25 * np.eye(window, k=1) + 0.25 * np.eye(window, k=-1)
    places = np.arange(window) - half
    for variant in range(4):
        keep = np.ones(window)
        if variant & 1:
            keep[places < 0] = 0.0
        if variant & 2:
            keep[places >= rows] = 0.0
        step = keep[:, None] * band * keep[None, :]
        scales = (step, np.linalg.matrix_power(step, COARSE))
        for scale, matrix in enumerate(scales):
            matrix = matrix[half : half + rows]
            for field in range(fields):
                at = (scale * fields + field) * rows
                out[variant, at : at + rows, field * rows : (field + 1) * rows] = matrix[:, half : half + rows]
                tile, part = field % pairs, field // pairs
                low = (fields + tile) * rows + part * half
                out[variant, at : at + rows, low : low + half] = matrix[:, :half]
                high = (fields + pairs + tile) * rows + part * half
                out[variant, at : at + rows, high : high + half] = matrix[:, half + rows :]
    return out


def split_dot(matrix, values, parts):
    pieces = []
    for _ in range(parts):
        piece = values.astype(jnp.bfloat16)
        pieces.append(piece)
        values = values - piece.astype(jnp.float32)
    return jnp.dot(matrix, jnp.concatenate(pieces, axis=0), preferred_element_type=jnp.float32)


def wrapped(tiles, width):
    whole = width // LANES
    rest = width - whole * LANES
    last = tiles[:, whole * LANES :]
    lane = lax.broadcasted_iota(jnp.int32, last.shape, 1)
    ahead = pltpu.roll(tiles[:, :LANES], rest, 1)
    behind = pltpu.roll(last, LANES - rest, 1)
    last = jnp.where(lane < rest, last, jnp.where(lane < (LANES + rest) // 2, ahead, behind))
    return jnp.concatenate([tiles[:, : whole * LANES], last], axis=1)


def lon_pass(tiles, passes):
    size = tiles.shape[1]
    total = math.comb(2 * passes, passes) / 4.0**passes * tiles
    for far in range(1, passes + 1):
        both = pltpu.roll(tiles, far, 1) + pltpu.roll(tiles, size - far, 1)
        total = total + math.comb(2 * passes, passes + far) / 4.0**passes * both
    return total


def lon_blur(ref, count, width):
    def step(field, carry):
        ref[field] = lon_pass(wrapped(ref[field], width), 1)
        ref[count + field] = lon_pass(wrapped(ref[count + field], width), COARSE)
        return carry

    lax.fori_loop(0, count, step, 0, unroll=4 if count % 4 == 0 else 2)


def slope(differ):
    return differ * lax.rsqrt(differ * differ + 0.01)


def kernel(
    dims,
    in_ref, obs_hbm, factor_ref, weight_hbm, band_hbm, back_hbm, obs_band_hbm,
    out_ref,
    main_ref, rest_ref, obs_ref, weight_ref, band_ref, back_ref, obs_band_ref,
    staged, fields, rests, rest_out, halo_out, obs_fields, obs_halo, obs_sm, smooth, result, result_rest,
    edge_out, edge_in,
    f_send, f_recv, fr_send, fr_recv, own_sem, stage_sem,
    h_send, h_recv, oh_send, oh_recv, e_send, e_recv,
    b_send, b_recv, br_send, br_recv, bown_sem, load_sem, out_sem,
):
    ens_n, lat_n, local, members, group, rows, width = dims
    half = rows // 2
    pairs = members // 2
    full = width // LANES * LANES
    rest = width - full
    padded = full + LANES
    total_rows = 2 * members * rows
    me = lax.axis_index("ens")
    lat = lax.axis_index("lat")
    has_low = lat > 0
    has_high = lat < lat_n - 1
    variant = (lat == 0).astype(jnp.int32) + 2 * (lat == lat_n - 1).astype(jnp.int32)

    def peer(shift):
        return lax.rem(me + shift, ens_n)

    barrier = pltpu.get_barrier_semaphore()
    for shift in range(1, ens_n):
        pl.semaphore_signal(barrier, inc=1, device_id={"ens": peer(shift)}, device_id_type=MESH)

    @pl.when(has_low)
    def _():
        pl.semaphore_signal(barrier, inc=1, device_id={"lat": lat - 1}, device_id_type=MESH)

    @pl.when(has_high)
    def _():
        pl.semaphore_signal(barrier, inc=1, device_id={"lat": lat + 1}, device_id_type=MESH)

    stage = pltpu.make_async_copy(in_ref, staged, stage_sem)
    stage.start()
    loads = [
        pltpu.make_async_copy(source, target, load_sem.at[i])
        for i, (source, target) in enumerate((
            (obs_hbm, obs_ref),
            (weight_hbm.at[lat], weight_ref),
            *((band_hbm.at[variant], band_ref.at[:, pl.ds(part * total_rows, total_rows)]) for part in range(3)),
            *((back_hbm.at[variant], back_ref.at[:, pl.ds(part * total_rows, total_rows)]) for part in range(2)),
            (obs_band_hbm.at[variant], obs_band_ref),
        ))
    ]
    for load in loads:
        load.start()

    def zero_edges(low):
        at = members if low else members + pairs
        side = 0 if low else 1

        def clear(k, carry):
            def tile(p, inner):
                fields[k, at + p] = jnp.zeros((rows, padded), jnp.float32)
                edge_in[k, side, p] = jnp.zeros((rows, padded), jnp.float32)
                return inner

            lax.fori_loop(0, pairs, tile, 0)
            return carry

        lax.fori_loop(0, group, clear, 0)
        obs_at = group if low else group + group // 2
        for p in range(group // 2):
            obs_fields[obs_at + p] = jnp.zeros((rows, padded), jnp.float32)

    @pl.when(jnp.logical_not(has_low))
    def _():
        zero_edges(True)

    @pl.when(jnp.logical_not(has_high))
    def _():
        zero_edges(False)

    pl.semaphore_wait(barrier, ens_n - 1 + has_low.astype(jnp.int32) + has_high.astype(jnp.int32))

    def f_main(k, shift):
        target = peer(shift)
        return pltpu.make_async_remote_copy(
            src_ref=in_ref.at[:, target * group + k, :, pl.ds(0, full)],
            dst_ref=fields.at[k, pl.ds(me * local, local), :, pl.ds(0, full)],
            send_sem=f_send.at[k, shift], recv_sem=f_recv.at[k, shift],
            device_id={"ens": target}, device_id_type=MESH,
        )

    def f_rest(k, shift):
        target = peer(shift)
        return pltpu.make_async_remote_copy(
            src_ref=rest_out.at[k, target], dst_ref=rests.at[k, me],
            send_sem=fr_send.at[k, shift], recv_sem=fr_recv.at[k, shift],
            device_id={"ens": target}, device_id_type=MESH,
        )

    def f_own(k):
        return pltpu.make_async_copy(
            in_ref.at[:, me * group + k, :, pl.ds(0, full)],
            fields.at[k, pl.ds(me * local, local), :, pl.ds(0, full)],
            own_sem.at[k],
        )

    def start_main(k):
        for shift in range(1, ens_n):
            f_main(k, shift).start()
        f_own(k).start()

    lane = lax.broadcasted_iota(jnp.int32, (rows, LANES), 1)

    def packed(tiles):
        total = tiles[0]
        for m in range(1, local):
            total = jnp.where(lane < m * rest, total, pltpu.roll(tiles[m], m * rest, 1))
        return total

    def start_rest(k):
        for target in range(ens_n):
            tile = packed([
                jnp.concatenate(
                    [staged[m, target * group + k, :, pl.ds(full, rest)],
                     jnp.zeros((rows, LANES - rest), jnp.float32)], axis=1)
                for m in range(local)
            ])
            rest_out[k, target] = tile
        rests[k, me] = rest_out[k, me]
        for shift in range(1, ens_n):
            f_rest(k, shift).start()

    ahead = min(2, group)
    start_main(0)
    stage.wait()
    start_rest(0)
    upper = lax.broadcasted_iota(jnp.int32, (rows, padded), 0) < half

    def turn(tile):
        return pltpu.roll(tile, half, 0)

    def neighbour_copies(source, targets, send, recv):
        return (
            pltpu.make_async_remote_copy(
                src_ref=source[0], dst_ref=targets[1], send_sem=send.at[0], recv_sem=recv.at[1],
                device_id={"lat": lat - 1}, device_id_type=MESH,
            ),
            pltpu.make_async_remote_copy(
                src_ref=source[1], dst_ref=targets[0], send_sem=send.at[1], recv_sem=recv.at[0],
                device_id={"lat": lat + 1}, device_id_type=MESH,
            ),
        )

    def start_both(copies):
        @pl.when(has_low)
        def _():
            copies[0].start()

        @pl.when(has_high)
        def _():
            copies[1].start()

    def recv_both(copies):
        @pl.when(has_low)
        def _():
            copies[1].wait_recv()

        @pl.when(has_high)
        def _():
            copies[0].wait_recv()

    def sent_both(copies):
        @pl.when(has_low)
        def _():
            copies[0].wait_send()

        @pl.when(has_high)
        def _():
            copies[1].wait_send()

    def halo_copies(k):
        return neighbour_copies(
            (halo_out.at[k, 0], halo_out.at[k, 1]),
            (fields.at[k, pl.ds(members, pairs)], fields.at[k, pl.ds(members + pairs, pairs)]),
            h_send.at[k], h_recv.at[k],
        )

    def edge_copies(k):
        return neighbour_copies(
            (edge_out.at[k, 0], edge_out.at[k, 1]), (edge_in.at[k, 0], edge_in.at[k, 1]),
            e_send.at[k], e_recv.at[k],
        )

    for load in loads:
        load.wait()
    couples = group // 2
    obs_copies = neighbour_copies(
        (obs_halo.at[0], obs_halo.at[1]),
        (obs_fields.at[pl.ds(group, couples)], obs_fields.at[pl.ds(group + couples, couples)]),
        oh_send, oh_recv,
    )
    for c in range(group):
        obs_fields[c, :, pl.ds(full, LANES)] = jnp.zeros((rows, LANES), jnp.float32)
        obs_fields[c, :, pl.ds(0, width)] = obs_ref[c]
    for p in range(couples):
        one, two = obs_fields[p], obs_fields[p + couples]
        obs_halo[0, p] = jnp.where(upper, one, turn(two))
        obs_halo[1, p] = jnp.where(upper, turn(one), two)
    start_both(obs_copies)
    recv_both(obs_copies)
    values = obs_fields[...].reshape(2 * group * rows, padded)
    obs_sm[...] = split_dot(obs_band_ref[...], values, 3).reshape(2 * group, rows, padded)
    lon_blur(obs_sm, group, width)
    for k in range(1, ahead):
        start_main(k)
        start_rest(k)

    def take_fields(k):
        for shift in range(1, ens_n):
            f_main(k, shift).wait_recv()
            f_rest(k, shift).wait_recv()
        f_own(k).wait()

        def unpack(source, carry):
            tile = rests[k, source]
            for m in range(local):
                fields[k, source * local + m, :, pl.ds(full, LANES)] = (
                    pltpu.roll(tile, LANES - m * rest, 1) if m else tile
                )
            return carry

        lax.fori_loop(0, ens_n, unpack, 0, unroll=True)

        def pack_halo(p, carry):
            one, two = fields[k, p], fields[k, p + pairs]
            halo_out[k, 0, p] = jnp.where(upper, one, turn(two))
            halo_out[k, 1, p] = jnp.where(upper, turn(one), two)
            return carry

        lax.fori_loop(0, pairs, pack_halo, 0, unroll=4 if pairs % 4 == 0 else 1)
        start_both(halo_copies(k))

        @pl.when(k + ahead < group)
        def _():
            start_main(k + ahead)
            start_rest(k + ahead)

    block = 2 * LANES if padded % (2 * LANES) == 0 else LANES

    def forward(k):
        recv_both(halo_copies(k))

        def smooth_block(b, carry):
            at = pl.ds(pl.multiple_of(b * block, block), block)
            values = fields[k, :, :, at].reshape(total_rows, block)
            smooth[:, :, at] = split_dot(band_ref[...], values, 3).reshape(2 * members, rows, block)
            return carry

        lax.fori_loop(0, padded // block, smooth_block, 0, unroll=3 if padded // block % 3 == 0 else 1)
        lon_blur(smooth, members, width)
        weight = factor_ref[me * group + k] * jnp.broadcast_to(weight_ref[:, :1], (rows, LANES))
        pull = 0.95 / (members - 1)
        tiles = padded // LANES

        def couple(i, carry):
            scale, t = i // tiles, i % tiles
            at = pl.ds(pl.multiple_of(t * LANES, LANES), LANES)
            base = scale * members
            held = [smooth[base + m, :, at] for m in range(members)]
            sums = [None] * members
            for m in range(members):
                for other in range(m):
                    force = slope(held[m] - held[other])
                    sums[m] = force if sums[m] is None else sums[m] + force
                    sums[other] = -force if sums[other] is None else sums[other] - force
            analysis = obs_sm[scale * group + k, :, at]
            for m in range(members):
                smooth[base + m, :, at] = weight * (slope(held[m] - analysis) - pull * sums[m])
            return carry

        lax.fori_loop(0, 2 * tiles, couple, 0)

    def backward(k):
        lon_blur(smooth, members, width)

        def back_block(b, carry):
            at = pl.ds(pl.multiple_of(b * block, block), block)
            values = smooth[:, :, at].reshape(total_rows, block)
            out = split_dot(back_ref[...], values, 2).reshape(2 * members, rows, block)
            result[k, :, :, at] = out[:members]
            edge_out[k, 0, :, :, at] = out[members : members + pairs]
            edge_out[k, 1, :, :, at] = out[members + pairs :]
            return carry

        lax.fori_loop(0, padded // block, back_block, 0, unroll=3 if padded // block % 3 == 0 else 1)
        start_both(edge_copies(k))

    def b_main(k, shift):
        target = peer(shift)
        return pltpu.make_async_remote_copy(
            src_ref=result.at[k, pl.ds(target * local, local), :, pl.ds(0, full)],
            dst_ref=main_ref.at[:, me * group + k, :, pl.ds(0, full)],
            send_sem=b_send.at[k, shift], recv_sem=b_recv.at[k, shift],
            device_id={"ens": target}, device_id_type=MESH,
        )

    def b_rest(k, shift):
        target = peer(shift)
        return pltpu.make_async_remote_copy(
            src_ref=result_rest.at[k, target], dst_ref=rest_ref.at[me * group + k],
            send_sem=br_send.at[k, shift], recv_sem=br_recv.at[k, shift],
            device_id={"ens": target}, device_id_type=MESH,
        )

    def b_own(k):
        return pltpu.make_async_copy(
            result.at[k, pl.ds(me * local, local), :, pl.ds(0, full)],
            main_ref.at[:, me * group + k, :, pl.ds(0, full)], bown_sem.at[k],
        )

    def write(k, source):
        channel = source * group + k
        return pltpu.make_async_copy(
            main_ref.at[:, channel], out_ref.at[:, channel], out_sem.at[k, source]
        )

    def finish(k):
        recv_both(edge_copies(k))

        def add(p, carry):
            low, high = edge_in[k, 0, p], edge_in[k, 1, p]
            result[k, p] = result[k, p] + jnp.where(upper, low, turn(high))
            result[k, p + pairs] = result[k, p + pairs] + jnp.where(upper, turn(low), high)
            return carry

        lax.fori_loop(0, pairs, add, 0, unroll=4 if pairs % 4 == 0 else 1)

        def pack(target, carry):
            result_rest[k, target] = packed(
                [result[k, target * local + m, :, pl.ds(full, LANES)] for m in range(local)]
            )
            return carry

        lax.fori_loop(0, ens_n, pack, 0, unroll=True)
        for shift in range(1, ens_n):
            b_main(k, shift).start()
            b_rest(k, shift).start()
        b_own(k).start()
        rest_ref[me * group + k] = result_rest[k, me]

    take_fields(0)

    def turn_of(k, carry):
        forward(k)

        @pl.when(k > 0)
        def _():
            finish(k - 1)

        @pl.when(k + 1 < group)
        def _():
            take_fields(k + 1)

        backward(k)

        return carry

    lax.fori_loop(0, group, turn_of, 0)
    finish(group - 1)

    sent_both(obs_copies)

    def drain(k, carry):
        for shift in range(1, ens_n):
            b_main(k, shift).wait_recv()
            b_rest(k, shift).wait_recv()
        b_own(k).wait()

        def unpack(source, inner):
            channel = source * group + k
            tile = rest_ref[channel]
            for m in range(local):
                main_ref[m, channel, :, pl.ds(full, rest)] = tile[:, m * rest : (m + 1) * rest]
            write(k, source).start()
            return inner

        lax.fori_loop(0, ens_n, unpack, 0)
        for shift in range(1, ens_n):
            f_main(k, shift).wait_send()
            f_rest(k, shift).wait_send()
            b_main(k, shift).wait_send()
            b_rest(k, shift).wait_send()
        sent_both(halo_copies(k))
        sent_both(edge_copies(k))
        return carry

    lax.fori_loop(0, group, drain, 0)

    def close(k, carry):
        for source in range(ens_n):
            write(k, source).wait()
        return carry

    lax.fori_loop(0, group, close, 0)


def body(prediction_array, verifying_analysis, variable_penalty_factor):
    local, channels, rows, width = prediction_array.shape
    group = verifying_analysis.shape[0]
    ens_n, lat_n = lax.axis_size("ens"), lax.axis_size("lat")
    members = local * ens_n
    pairs = members // 2
    full = width // LANES * LANES
    rest = width - full
    padded = full + LANES
    assert rows % 8 == 0 and rows // 2 >= COARSE and local * rest <= LANES and channels == group * ens_n
    assert members % 2 == 0 and group % 2 == 0 and LANES - rest >= 4 * COARSE

    bands = band_matrices(members, rows)
    band = jnp.asarray(bands, jnp.bfloat16)
    back = jnp.asarray(bands.transpose(0, 2, 1), jnp.bfloat16)
    square = bands.shape[1]
    obs_bands = band_matrices(group, rows)
    obs_band = jnp.asarray(np.concatenate([obs_bands] * 3, axis=2), jnp.bfloat16)
    ids = np.arange(lat_n * rows).astype(np.float32)
    degrees = np.float32(0.25) * (ids - np.float32((lat_n * rows - 1) / 2.0))
    weights = np.cos(degrees * np.float32(np.pi / 180.0)).astype(np.float32).reshape(lat_n, rows, 1)
    weights = jnp.asarray(np.pad(weights, ((0, 0), (0, 0), (0, LANES - 1))))

    dims = (ens_n, lat_n, local, members, group, rows, width)
    hbm = pl.BlockSpec(memory_space=pl.ANY)
    f32 = jnp.float32
    dma = pltpu.SemaphoreType.DMA
    cells = group * padded * rows
    return pl.pallas_call(
        functools.partial(kernel, dims),
        out_shape=jax.ShapeDtypeStruct((local, channels, rows, width), f32),
        in_specs=[hbm, hbm, pl.BlockSpec(memory_space=pltpu.SMEM), hbm, hbm, hbm, hbm],
        out_specs=hbm,
        scratch_shapes=[
            pltpu.VMEM((local, channels, rows, width), f32),
            pltpu.VMEM((channels, rows, LANES), f32),
            pltpu.VMEM(verifying_analysis.shape, f32),
            pltpu.VMEM(weights.shape[1:], f32),
            pltpu.VMEM((square, 3 * square), jnp.bfloat16),
            pltpu.VMEM((square, 2 * square), jnp.bfloat16),
            pltpu.VMEM(obs_band.shape[1:], jnp.bfloat16),
            pltpu.VMEM((local, channels, rows, width), f32),
            pltpu.VMEM((group, members + 2 * pairs, rows, padded), f32),
            pltpu.VMEM((group, ens_n, rows, LANES), f32),
            pltpu.VMEM((group, ens_n, rows, LANES), f32),
            pltpu.VMEM((group, 2, pairs, rows, padded), f32),
            pltpu.VMEM((2 * group, rows, padded), f32),
            pltpu.VMEM((2, group // 2, rows, padded), f32),
            pltpu.VMEM((2 * group, rows, padded), f32),
            pltpu.VMEM((2 * members, rows, padded), f32),
            pltpu.VMEM((group, members, rows, padded), f32),
            pltpu.VMEM((group, ens_n, rows, LANES), f32),
            pltpu.VMEM((group, 2, pairs, rows, padded), f32),
            pltpu.VMEM((group, 2, pairs, rows, padded), f32),
            dma((group, ens_n)), dma((group, ens_n)), dma((group, ens_n)), dma((group, ens_n)),
            dma((group,)), dma,
            dma((group, 2)), dma((group, 2)), dma((2,)), dma((2,)), dma((group, 2)), dma((group, 2)),
            dma((group, ens_n)), dma((group, ens_n)), dma((group, ens_n)), dma((group, ens_n)),
            dma((group,)), dma((8,)), dma((group, ens_n)),
        ],
        compiler_params=pltpu.CompilerParams(
            collective_id=0, has_side_effects=True, vmem_limit_bytes=62 * 1024 * 1024
        ),
        cost_estimate=pl.CostEstimate(
            flops=cells * members * members * 6, bytes_accessed=cells * members * 8,
            transcendentals=cells * members * members,
        ),
    )(prediction_array, verifying_analysis, variable_penalty_factor, weights, band, back, obs_band)


def solution(mesh):
    placed = (P("ens", None, "lat", None), P("ens", "lat", None), P())
    return jax.shard_map(
        body, mesh=mesh, in_specs=placed, out_specs=P("ens", None, "lat", None), check_vma=False
    )
```

```python
import functools
import math

import jax
import jax.numpy as jnp
import numpy as np
from jax import lax
from jax.experimental import pallas as pl
from jax.experimental.pallas import tpu as pltpu
from jax.sharding import PartitionSpec as P

COARSE = 3
LANES = 128
COPIES = 4
GRANT = 62 * 1024 * 1024
MESH = pl.DeviceIdType.MESH


def round_up(value, unit):
    return -(-value // unit) * unit


def band_matrices(fields, rows):
    half = rows // 2
    pairs = fields // 2
    out = np.zeros((4, 2 * fields * rows, 2 * fields * rows), np.float32)
    window = 2 * rows
    band = 0.5 * np.eye(window) + 0.25 * np.eye(window, k=1) + 0.25 * np.eye(window, k=-1)
    places = np.arange(window) - half
    for variant in range(4):
        keep = np.ones(window)
        if variant & 1:
            keep[places < 0] = 0.0
        if variant & 2:
            keep[places >= rows] = 0.0
        step = keep[:, None] * band * keep[None, :]
        scales = (step, np.linalg.matrix_power(step, COARSE))
        for scale, matrix in enumerate(scales):
            matrix = matrix[half : half + rows]
            for field in range(fields):
                at = (scale * fields + field) * rows
                out[variant, at : at + rows, field * rows : (field + 1) * rows] = matrix[:, half : half + rows]
                tile, part = field % pairs, field // pairs
                low = (fields + tile) * rows + part * half
                out[variant, at : at + rows, low : low + half] = matrix[:, :half]
                high = (fields + pairs + tile) * rows + part * half
                out[variant, at : at + rows, high : high + half] = matrix[:, half + rows :]
    return out


def split_dot(matrix, values, parts):
    pieces = []
    for _ in range(parts):
        piece = values.astype(jnp.bfloat16)
        pieces.append(piece)
        values = values - piece.astype(jnp.float32)
    return jnp.dot(matrix, jnp.concatenate(pieces, axis=0), preferred_element_type=jnp.float32)


def wrapped(tiles, width):
    whole = width // LANES
    rest = width - whole * LANES
    last = tiles[:, whole * LANES :]
    lane = lax.broadcasted_iota(jnp.int32, last.shape, 1)
    ahead = pltpu.roll(tiles[:, :LANES], rest, 1)
    behind = pltpu.roll(last, LANES - rest, 1)
    last = jnp.where(lane < rest, last, jnp.where(lane < (LANES + rest) // 2, ahead, behind))
    return jnp.concatenate([tiles[:, : whole * LANES], last], axis=1)


def lon_pass(tiles, passes):
    size = tiles.shape[1]
    total = math.comb(2 * passes, passes) / 4.0**passes * tiles
    for far in range(1, passes + 1):
        both = pltpu.roll(tiles, far, 1) + pltpu.roll(tiles, size - far, 1)
        total = total + math.comb(2 * passes, passes + far) / 4.0**passes * both
    return total


def lon_blur(ref, count, width):
    def step(field, carry):
        ref[field] = lon_pass(wrapped(ref[field], width), 1)
        ref[count + field] = lon_pass(wrapped(ref[count + field], width), COARSE)
        return carry

    lax.fori_loop(0, count, step, 0, unroll=4 if count % 4 == 0 else 2)


def slope(differ):
    return differ * lax.rsqrt(differ * differ + 0.01)


def kernel(
    dims,
    in_ref, obs_hbm, factor_ref, weight_hbm, band_hbm, back_hbm, obs_band_hbm,
    out_ref,
    main_ref, rest_ref, obs_ref, weight_ref, band_ref, back_ref, obs_band_ref,
    staged, fields, rests, rest_out, halo_out, obs_fields, obs_halo, obs_sm, smooth, result, result_rest,
    edge_out, edge_in,
    f_send, f_recv, fr_send, fr_recv, own_sem, stage_sem,
    h_send, h_recv, oh_send, oh_recv, e_send, e_recv,
    b_send, b_recv, br_send, br_recv, bown_sem, load_sem, out_sem,
):
    ens_n, lat_n, local, members, group, rows, width = dims
    half = rows // 2
    pairs = members // 2
    full = width // LANES * LANES
    rest = width - full
    padded = full + LANES
    total_rows = 2 * members * rows
    me = lax.axis_index("ens")
    lat = lax.axis_index("lat")
    has_low = lat > 0
    has_high = lat < lat_n - 1
    variant = (lat == 0).astype(jnp.int32) + 2 * (lat == lat_n - 1).astype(jnp.int32)

    def peer(shift):
        return lax.rem(me + shift, ens_n)

    barrier = pltpu.get_barrier_semaphore()
    for shift in range(1, ens_n):
        pl.semaphore_signal(barrier, inc=1, device_id={"ens": peer(shift)}, device_id_type=MESH)

    @pl.when(has_low)
    def _():
        pl.semaphore_signal(barrier, inc=1, device_id={"lat": lat - 1}, device_id_type=MESH)

    @pl.when(has_high)
    def _():
        pl.semaphore_signal(barrier, inc=1, device_id={"lat": lat + 1}, device_id_type=MESH)

    stage = pltpu.make_async_copy(in_ref, staged, stage_sem)
    stage.start()
    loads = [
        pltpu.make_async_copy(source, target, load_sem.at[i])
        for i, (source, target) in enumerate((
            (obs_hbm, obs_ref),
            (weight_hbm.at[lat], weight_ref),
            *((band_hbm.at[variant], band_ref.at[:, pl.ds(part * total_rows, total_rows)]) for part in range(3)),
            *((back_hbm.at[variant], back_ref.at[:, pl.ds(part * total_rows, total_rows)]) for part in range(2)),
            (obs_band_hbm.at[variant], obs_band_ref),
        ))
    ]
    for load in loads:
        load.start()

    def zero_edges(low):
        at = members if low else members + pairs
        side = 0 if low else 1

        def clear(k, carry):
            def tile(p, inner):
                fields[k, at + p] = jnp.zeros((rows, padded), jnp.float32)
                edge_in[k, side, p] = jnp.zeros((rows, padded), jnp.float32)
                return inner

            lax.fori_loop(0, pairs, tile, 0)
            return carry

        lax.fori_loop(0, group, clear, 0)
        obs_at = group if low else group + group // 2
        for p in range(group // 2):
            obs_fields[obs_at + p] = jnp.zeros((rows, padded), jnp.float32)

    pl.semaphore_wait(barrier, ens_n - 1 + has_low.astype(jnp.int32) + has_high.astype(jnp.int32))

    def f_main(k, shift):
        target = peer(shift)
        return pltpu.make_async_remote_copy(
            src_ref=in_ref.at[:, target * group + k, :, pl.ds(0, full)],
            dst_ref=fields.at[k, pl.ds(me * local, local), :, pl.ds(0, full)],
            send_sem=f_send.at[k, shift], recv_sem=f_recv.at[k, shift],
            device_id={"ens": target}, device_id_type=MESH,
        )

    def f_rest(shift):
        target = peer(shift)
        return pltpu.make_async_remote_copy(
            src_ref=rest_out.at[target], dst_ref=rests.at[me],
            send_sem=fr_send.at[shift], recv_sem=fr_recv.at[shift],
            device_id={"ens": target}, device_id_type=MESH,
        )

    def f_own(k):
        return pltpu.make_async_copy(
            in_ref.at[:, me * group + k, :, pl.ds(0, full)],
            fields.at[k, pl.ds(me * local, local), :, pl.ds(0, full)],
            own_sem.at[k],
        )

    def start_main(k):
        for shift in range(1, ens_n):
            f_main(k, shift).start()
        f_own(k).start()

    lane = lax.broadcasted_iota(jnp.int32, (rows, LANES), 1)

    def packed(tiles):
        total = tiles[0]
        for m in range(1, local):
            total = jnp.where(lane < m * rest, total, pltpu.roll(tiles[m], m * rest, 1))
        return total

    def pack_rest(target, carry):
        for k in range(group):
            rest_out[target, k] = packed([
                jnp.concatenate(
                    [staged[m, target * group + k, :, pl.ds(full, rest)],
                     jnp.zeros((rows, LANES - rest), jnp.float32)], axis=1)
                for m in range(local)
            ])
        return carry

    ahead = min(2, group)
    start_main(0)

    @pl.when(jnp.logical_not(has_low))
    def _():
        zero_edges(True)

    @pl.when(jnp.logical_not(has_high))
    def _():
        zero_edges(False)

    stage.wait()
    lax.fori_loop(0, ens_n, pack_rest, 0)
    rests[me] = rest_out[me]
    for shift in range(1, ens_n):
        f_rest(shift).start()

    upper = lax.broadcasted_iota(jnp.int32, (rows, padded), 0) < half

    def turn(tile):
        return pltpu.roll(tile, half, 0)

    def neighbour_copies(source, targets, send, recv):
        return (
            pltpu.make_async_remote_copy(
                src_ref=source[0], dst_ref=targets[1], send_sem=send.at[0], recv_sem=recv.at[1],
                device_id={"lat": lat - 1}, device_id_type=MESH,
            ),
            pltpu.make_async_remote_copy(
                src_ref=source[1], dst_ref=targets[0], send_sem=send.at[1], recv_sem=recv.at[0],
                device_id={"lat": lat + 1}, device_id_type=MESH,
            ),
        )

    def start_both(copies):
        @pl.when(has_low)
        def _():
            copies[0].start()

        @pl.when(has_high)
        def _():
            copies[1].start()

    def recv_both(copies):
        @pl.when(has_low)
        def _():
            copies[1].wait_recv()

        @pl.when(has_high)
        def _():
            copies[0].wait_recv()

    def sent_both(copies):
        @pl.when(has_low)
        def _():
            copies[0].wait_send()

        @pl.when(has_high)
        def _():
            copies[1].wait_send()

    def halo_copies(k):
        return neighbour_copies(
            (halo_out.at[k, 0], halo_out.at[k, 1]),
            (fields.at[k, pl.ds(members, pairs)], fields.at[k, pl.ds(members + pairs, pairs)]),
            h_send.at[k], h_recv.at[k],
        )

    def edge_copies(k):
        return neighbour_copies(
            (edge_out.at[k, 0], edge_out.at[k, 1]), (edge_in.at[k, 0], edge_in.at[k, 1]),
            e_send.at[k], e_recv.at[k],
        )

    for load in loads:
        load.wait()
    couples = group // 2
    obs_copies = neighbour_copies(
        (obs_halo.at[0], obs_halo.at[1]),
        (obs_fields.at[pl.ds(group, couples)], obs_fields.at[pl.ds(group + couples, couples)]),
        oh_send, oh_recv,
    )
    for c in range(group):
        obs_fields[c, :, pl.ds(full, LANES)] = jnp.zeros((rows, LANES), jnp.float32)
        obs_fields[c, :, pl.ds(0, width)] = obs_ref[c]
    for p in range(couples):
        one, two = obs_fields[p], obs_fields[p + couples]
        obs_halo[0, p] = jnp.where(upper, one, turn(two))
        obs_halo[1, p] = jnp.where(upper, turn(one), two)
    start_both(obs_copies)
    recv_both(obs_copies)
    values = obs_fields[...].reshape(2 * group * rows, padded)
    obs_sm[...] = split_dot(obs_band_ref[...], values, 3).reshape(2 * group, rows, padded)
    lon_blur(obs_sm, group, width)
    for k in range(1, ahead):
        start_main(k)

    def take_fields(k):
        for shift in range(1, ens_n):
            f_main(k, shift).wait_recv()
        f_own(k).wait()

        def unpack(source, carry):
            tile = rests[source, k]
            for m in range(local):
                fields[k, source * local + m, :, pl.ds(full, LANES)] = (
                    pltpu.roll(tile, LANES - m * rest, 1) if m else tile
                )
            return carry

        lax.fori_loop(0, ens_n, unpack, 0, unroll=True)

        def pack_halo(p, carry):
            one, two = fields[k, p], fields[k, p + pairs]
            halo_out[k, 0, p] = jnp.where(upper, one, turn(two))
            halo_out[k, 1, p] = jnp.where(upper, turn(one), two)
            return carry

        lax.fori_loop(0, pairs, pack_halo, 0, unroll=4 if pairs % 4 == 0 else 1)
        start_both(halo_copies(k))

        @pl.when(k + ahead < group)
        def _():
            start_main(k + ahead)

    block = 2 * LANES if padded % (2 * LANES) == 0 else LANES

    def forward(k):
        recv_both(halo_copies(k))

        def smooth_block(b, carry):
            at = pl.ds(pl.multiple_of(b * block, block), block)
            values = fields[k, :, :, at].reshape(total_rows, block)
            smooth[:, :, at] = split_dot(band_ref[...], values, 3).reshape(2 * members, rows, block)
            return carry

        lax.fori_loop(0, padded // block, smooth_block, 0, unroll=3 if padded // block % 3 == 0 else 1)
        lon_blur(smooth, members, width)

    def interact(k):
        weight = factor_ref[me * group + k] * jnp.broadcast_to(weight_ref[:, :1], (rows, LANES))
        pull = 0.95 / (members - 1)
        tiles = padded // LANES

        def couple(i, carry):
            scale, t = i // tiles, i % tiles
            at = pl.ds(pl.multiple_of(t * LANES, LANES), LANES)
            base = scale * members
            held = [smooth[base + m, :, at] for m in range(members)]
            sums = [None] * members
            for m in range(members):
                for other in range(m):
                    force = slope(held[m] - held[other])
                    sums[m] = force if sums[m] is None else sums[m] + force
                    sums[other] = -force if sums[other] is None else sums[other] - force
            analysis = obs_sm[scale * group + k, :, at]
            for m in range(members):
                smooth[base + m, :, at] = weight * (slope(held[m] - analysis) - pull * sums[m])
            return carry

        lax.fori_loop(0, 2 * tiles, couple, 0)

    def backward(k):
        lon_blur(smooth, members, width)

        def back_block(b, carry):
            at = pl.ds(pl.multiple_of(b * block, block), block)
            values = smooth[:, :, at].reshape(total_rows, block)
            out = split_dot(back_ref[...], values, 2).reshape(2 * members, rows, block)
            result[k, :, :, at] = out[:members]
            edge_out[k, 0, :, :, at] = out[members : members + pairs]
            edge_out[k, 1, :, :, at] = out[members + pairs :]
            return carry

        lax.fori_loop(0, padded // block, back_block, 0, unroll=3 if padded // block % 3 == 0 else 1)
        start_both(edge_copies(k))

    def b_main(k, shift):
        target = peer(shift)
        return pltpu.make_async_remote_copy(
            src_ref=result.at[k, pl.ds(target * local, local), :, pl.ds(0, full)],
            dst_ref=main_ref.at[:, me * group + k, :, pl.ds(0, full)],
            send_sem=b_send.at[k, shift], recv_sem=b_recv.at[k, shift],
            device_id={"ens": target}, device_id_type=MESH,
        )

    def b_rest(shift):
        target = peer(shift)
        return pltpu.make_async_remote_copy(
            src_ref=result_rest.at[target], dst_ref=rest_ref.at[pl.ds(me * group, group)],
            send_sem=br_send.at[shift], recv_sem=br_recv.at[shift],
            device_id={"ens": target}, device_id_type=MESH,
        )

    def b_own(k):
        return pltpu.make_async_copy(
            result.at[k, pl.ds(me * local, local), :, pl.ds(0, full)],
            main_ref.at[:, me * group + k, :, pl.ds(0, full)], bown_sem.at[k],
        )

    def write(k, source):
        channel = source * group + k
        return pltpu.make_async_copy(
            main_ref.at[:, channel], out_ref.at[:, channel], out_sem.at[k, source]
        )

    def finish(k):
        recv_both(edge_copies(k))

        def add(p, carry):
            low, high = edge_in[k, 0, p], edge_in[k, 1, p]
            result[k, p] = result[k, p] + jnp.where(upper, low, turn(high))
            result[k, p + pairs] = result[k, p + pairs] + jnp.where(upper, turn(low), high)
            return carry

        lax.fori_loop(0, pairs, add, 0, unroll=4 if pairs % 4 == 0 else 1)

        def pack(target, carry):
            result_rest[target, k] = packed(
                [result[k, target * local + m, :, pl.ds(full, LANES)] for m in range(local)]
            )
            return carry

        lax.fori_loop(0, ens_n, pack, 0, unroll=True)
        for shift in range(1, ens_n):
            b_main(k, shift).start()
        b_own(k).start()

    for shift in range(1, ens_n):
        f_rest(shift).wait_recv()
    take_fields(0)

    def turn_of(k, carry):
        forward(k)

        @pl.when(k + 1 < group)
        def _():
            take_fields(k + 1)

        interact(k)

        @pl.when(k > 0)
        def _():
            finish(k - 1)

        backward(k)

        return carry

    lax.fori_loop(0, group, turn_of, 0)
    finish(group - 1)
    for shift in range(1, ens_n):
        b_rest(shift).start()
    rest_ref[pl.ds(me * group, group)] = result_rest[me]

    sent_both(obs_copies)

    def drain(k, carry):
        for shift in range(1, ens_n):
            f_main(k, shift).wait_send()
        sent_both(halo_copies(k))
        sent_both(edge_copies(k))
        return carry

    lax.fori_loop(0, group, drain, 0)
    for shift in range(1, ens_n):
        f_rest(shift).wait_send()
        b_rest(shift).wait()

    def collect(k, carry):
        for shift in range(1, ens_n):
            b_main(k, shift).wait()
        b_own(k).wait()

        def unpack(source, inner):
            channel = source * group + k
            tile = rest_ref[channel]
            for m in range(local):
                main_ref[m, channel, :, pl.ds(full, rest)] = tile[:, m * rest : (m + 1) * rest]
            write(k, source).start()
            return inner

        lax.fori_loop(0, ens_n, unpack, 0, unroll=True)
        return carry

    lax.fori_loop(0, group, collect, 0)

    def close(k, carry):
        for source in range(ens_n):
            write(k, source).wait()
        return carry

    lax.fori_loop(0, group, close, 0)


def pass_on(in_ref, out_ref, sem):
    local, channels = in_ref.shape[:2]
    size = channels // COPIES
    copies = [
        pltpu.make_async_copy(
            in_ref.at[m, pl.ds(part * size, size)], out_ref.at[m, pl.ds(part * size, size)], sem.at[m, part]
        )
        for m in range(local)
        for part in range(COPIES)
    ]
    for copy in copies:
        copy.start()
    for copy in copies:
        copy.wait()


def body(prediction_array, verifying_analysis, variable_penalty_factor):
    local, channels, rows, width = prediction_array.shape
    group = verifying_analysis.shape[0]
    ens_n, lat_n = lax.axis_size("ens"), lax.axis_size("lat")
    members = local * ens_n
    pairs = members // 2
    full = width // LANES * LANES
    rest = width - full
    padded = full + LANES
    assert rows % 8 == 0 and rows // 2 >= COARSE and local * rest <= LANES and channels == group * ens_n
    assert members % 2 == 0 and group % 2 == 0 and LANES - rest >= 4 * COARSE

    bands = band_matrices(members, rows)
    band = jnp.asarray(bands, jnp.bfloat16)
    back = jnp.asarray(bands.transpose(0, 2, 1), jnp.bfloat16)
    square = bands.shape[1]
    obs_bands = band_matrices(group, rows)
    obs_band = jnp.asarray(np.concatenate([obs_bands] * 3, axis=2), jnp.bfloat16)
    ids = np.arange(lat_n * rows).astype(np.float32)
    degrees = np.float32(0.25) * (ids - np.float32((lat_n * rows - 1) / 2.0))
    weights = np.cos(degrees * np.float32(np.pi / 180.0)).astype(np.float32).reshape(lat_n, rows, 1)
    weights = jnp.asarray(np.pad(weights, ((0, 0), (0, 0), (0, LANES - 1))))

    dims = (ens_n, lat_n, local, members, group, rows, width)
    hbm = pl.BlockSpec(memory_space=pltpu.HBM)
    f32 = jnp.float32
    dma = pltpu.SemaphoreType.DMA
    cells = group * padded * rows
    gathered = pl.pallas_call(
        functools.partial(kernel, dims),
        out_shape=jax.ShapeDtypeStruct((local, channels, rows, width), f32),
        in_specs=[hbm, hbm, pl.BlockSpec(memory_space=pltpu.SMEM), hbm, hbm, hbm, hbm],
        out_specs=pl.BlockSpec(memory_space=pl.ANY),
        scratch_shapes=[
            pltpu.VMEM((local, channels, rows, width), f32),
            pltpu.VMEM((channels, rows, LANES), f32),
            pltpu.VMEM(verifying_analysis.shape, f32),
            pltpu.VMEM(weights.shape[1:], f32),
            pltpu.VMEM((square, 3 * square), jnp.bfloat16),
            pltpu.VMEM((square, 2 * square), jnp.bfloat16),
            pltpu.VMEM(obs_band.shape[1:], jnp.bfloat16),
            pltpu.VMEM((local, channels, rows, width), f32),
            pltpu.VMEM((group, members + 2 * pairs, rows, padded), f32),
            pltpu.VMEM((ens_n, group, rows, LANES), f32),
            pltpu.VMEM((ens_n, group, rows, LANES), f32),
            pltpu.VMEM((group, 2, pairs, rows, padded), f32),
            pltpu.VMEM((2 * group, rows, padded), f32),
            pltpu.VMEM((2, group // 2, rows, padded), f32),
            pltpu.VMEM((2 * group, rows, padded), f32),
            pltpu.VMEM((2 * members, rows, padded), f32),
            pltpu.VMEM((group, members, rows, padded), f32),
            pltpu.VMEM((ens_n, group, rows, LANES), f32),
            pltpu.VMEM((group, 2, pairs, rows, padded), f32),
            pltpu.VMEM((group, 2, pairs, rows, padded), f32),
            dma((group, ens_n)), dma((group, ens_n)), dma((ens_n,)), dma((ens_n,)),
            dma((group,)), dma,
            dma((group, 2)), dma((group, 2)), dma((2,)), dma((2,)), dma((group, 2)), dma((group, 2)),
            dma((group, ens_n)), dma((group, ens_n)), dma((ens_n,)), dma((ens_n,)),
            dma((group,)), dma((8,)), dma((group, ens_n)),
        ],
        compiler_params=pltpu.CompilerParams(
            collective_id=0, has_side_effects=True, vmem_limit_bytes=GRANT
        ),
        cost_estimate=pl.CostEstimate(
            flops=cells * members * members * 6, bytes_accessed=cells * members * 8,
            transcendentals=cells * members * members,
        ),
    )(prediction_array, verifying_analysis, variable_penalty_factor, weights, band, back, obs_band)
    return pl.pallas_call(
        pass_on,
        out_shape=jax.ShapeDtypeStruct(gathered.shape, f32),
        in_specs=[hbm],
        out_specs=hbm,
        scratch_shapes=[dma((local, COPIES))],
        compiler_params=pltpu.CompilerParams(vmem_limit_bytes=GRANT),
    )(gathered)


def solution(mesh):
    placed = (P("ens", None, "lat", None), P("ens", "lat", None), P())
    return jax.shard_map(
        body, mesh=mesh, in_specs=placed, out_specs=P("ens", None, "lat", None), check_vma=False
    )
```

```python
import functools
import math

import jax
import jax.numpy as jnp
import numpy as np
from jax import lax
from jax.experimental import pallas as pl
from jax.experimental.pallas import tpu as pltpu
from jax.sharding import PartitionSpec as P

COARSE = 3
LANES = 128
COPIES = 4
GRANT = 62 * 1024 * 1024
MESH = pl.DeviceIdType.MESH


def round_up(value, unit):
    return -(-value // unit) * unit


def band_matrices(fields, rows):
    half = rows // 2
    pairs = fields // 2
    out = np.zeros((4, 2 * fields * rows, 2 * fields * rows), np.float32)
    window = 2 * rows
    band = 0.5 * np.eye(window) + 0.25 * np.eye(window, k=1) + 0.25 * np.eye(window, k=-1)
    places = np.arange(window) - half
    for variant in range(4):
        keep = np.ones(window)
        if variant & 1:
            keep[places < 0] = 0.0
        if variant & 2:
            keep[places >= rows] = 0.0
        step = keep[:, None] * band * keep[None, :]
        scales = (step, np.linalg.matrix_power(step, COARSE))
        for scale, matrix in enumerate(scales):
            matrix = matrix[half : half + rows]
            for field in range(fields):
                at = (scale * fields + field) * rows
                out[variant, at : at + rows, field * rows : (field + 1) * rows] = matrix[:, half : half + rows]
                tile, part = field % pairs, field // pairs
                low = (fields + tile) * rows + part * half
                out[variant, at : at + rows, low : low + half] = matrix[:, :half]
                high = (fields + pairs + tile) * rows + part * half
                out[variant, at : at + rows, high : high + half] = matrix[:, half + rows :]
    return out


def split_dot(matrix, values, parts):
    pieces = []
    for _ in range(parts):
        piece = values.astype(jnp.bfloat16)
        pieces.append(piece)
        values = values - piece.astype(jnp.float32)
    return jnp.dot(matrix, jnp.concatenate(pieces, axis=0), preferred_element_type=jnp.float32)


def wrapped(tiles, width):
    whole = width // LANES
    rest = width - whole * LANES
    last = tiles[:, whole * LANES :]
    lane = lax.broadcasted_iota(jnp.int32, last.shape, 1)
    ahead = pltpu.roll(tiles[:, :LANES], rest, 1)
    behind = pltpu.roll(last, LANES - rest, 1)
    last = jnp.where(lane < rest, last, jnp.where(lane < (LANES + rest) // 2, ahead, behind))
    return jnp.concatenate([tiles[:, : whole * LANES], last], axis=1)


def lon_pass(tiles, passes):
    size = tiles.shape[1]
    total = math.comb(2 * passes, passes) / 4.0**passes * tiles
    for far in range(1, passes + 1):
        both = pltpu.roll(tiles, far, 1) + pltpu.roll(tiles, size - far, 1)
        total = total + math.comb(2 * passes, passes + far) / 4.0**passes * both
    return total


def lon_blur(ref, count, width):
    def step(field, carry):
        ref[field] = lon_pass(wrapped(ref[field], width), 1)
        ref[count + field] = lon_pass(wrapped(ref[count + field], width), COARSE)
        return carry

    lax.fori_loop(0, count, step, 0, unroll=4 if count % 4 == 0 else 2)


def slope(differ):
    return differ * lax.rsqrt(differ * differ + 0.01)


def kernel(
    dims,
    in_ref, obs_hbm, factor_ref, weight_hbm, band_hbm, back_hbm, obs_band_hbm,
    out_ref,
    main_ref, rest_ref, obs_ref, weight_ref, band_ref, back_ref, obs_band_ref,
    staged, fields, rests, rest_out, halo_out, obs_fields, obs_halo, obs_sm, smooth, result, result_rest,
    edge_out, edge_in,
    f_send, f_recv, fr_send, fr_recv, own_sem, stage_sem,
    h_send, h_recv, oh_send, oh_recv, e_send, e_recv,
    b_send, b_recv, br_send, br_recv, bown_sem, load_sem, out_sem,
):
    ens_n, lat_n, local, members, group, rows, width = dims
    half = rows // 2
    pairs = members // 2
    full = width // LANES * LANES
    rest = width - full
    padded = full + LANES
    total_rows = 2 * members * rows
    block = 2 * LANES if padded % (2 * LANES) == 0 else LANES
    cut = (padded // block + 1) // 2 * block
    ranges = ((0, cut), (cut, padded))
    last = len(ranges) - 1
    me = lax.axis_index("ens")
    lat = lax.axis_index("lat")
    has_low = lat > 0
    has_high = lat < lat_n - 1
    variant = (lat == 0).astype(jnp.int32) + 2 * (lat == lat_n - 1).astype(jnp.int32)

    def peer(shift):
        return lax.rem(me + shift, ens_n)

    barrier = pltpu.get_barrier_semaphore()
    for shift in range(1, ens_n):
        pl.semaphore_signal(barrier, inc=1, device_id={"ens": peer(shift)}, device_id_type=MESH)

    @pl.when(has_low)
    def _():
        pl.semaphore_signal(barrier, inc=1, device_id={"lat": lat - 1}, device_id_type=MESH)

    @pl.when(has_high)
    def _():
        pl.semaphore_signal(barrier, inc=1, device_id={"lat": lat + 1}, device_id_type=MESH)

    stage = pltpu.make_async_copy(in_ref, staged, stage_sem)
    stage.start()
    loads = [
        pltpu.make_async_copy(source, target, load_sem.at[i])
        for i, (source, target) in enumerate((
            (obs_hbm, obs_ref),
            (weight_hbm.at[lat], weight_ref),
            *((band_hbm.at[variant], band_ref.at[:, pl.ds(part * total_rows, total_rows)]) for part in range(3)),
            *((back_hbm.at[variant], back_ref.at[:, pl.ds(part * total_rows, total_rows)]) for part in range(2)),
            (obs_band_hbm.at[variant], obs_band_ref),
        ))
    ]
    for load in loads:
        load.start()

    def zero_edges(low):
        at = members if low else members + pairs
        side = 0 if low else 1

        def clear(k, carry):
            def tile(p, inner):
                fields[k, at + p] = jnp.zeros((rows, padded), jnp.float32)
                edge_in[k, side, p] = jnp.zeros((rows, padded), jnp.float32)
                return inner

            lax.fori_loop(0, pairs, tile, 0)
            return carry

        lax.fori_loop(0, group, clear, 0)
        obs_at = group if low else group + group // 2
        for p in range(group // 2):
            obs_fields[obs_at + p] = jnp.zeros((rows, padded), jnp.float32)

    pl.semaphore_wait(barrier, ens_n - 1 + has_low.astype(jnp.int32) + has_high.astype(jnp.int32))

    def sent_lanes(h):
        low, high = ranges[h]
        return pl.ds(low, min(high, full) - low)

    def f_main(k, h, shift):
        target = peer(shift)
        return pltpu.make_async_remote_copy(
            src_ref=in_ref.at[:, target * group + k, :, sent_lanes(h)],
            dst_ref=fields.at[k, pl.ds(me * local, local), :, sent_lanes(h)],
            send_sem=f_send.at[k, h, shift], recv_sem=f_recv.at[k, h, shift],
            device_id={"ens": target}, device_id_type=MESH,
        )

    def f_rest(shift):
        target = peer(shift)
        return pltpu.make_async_remote_copy(
            src_ref=rest_out.at[target], dst_ref=rests.at[me],
            send_sem=fr_send.at[shift], recv_sem=fr_recv.at[shift],
            device_id={"ens": target}, device_id_type=MESH,
        )

    def f_own(k):
        return pltpu.make_async_copy(
            in_ref.at[:, me * group + k, :, pl.ds(0, full)],
            fields.at[k, pl.ds(me * local, local), :, pl.ds(0, full)],
            own_sem.at[k],
        )

    def start_main(k):
        for h in range(len(ranges)):
            for shift in range(1, ens_n):
                f_main(k, h, shift).start()
        f_own(k).start()

    lane = lax.broadcasted_iota(jnp.int32, (rows, LANES), 1)

    def packed(tiles):
        total = tiles[0]
        for m in range(1, local):
            total = jnp.where(lane < m * rest, total, pltpu.roll(tiles[m], m * rest, 1))
        return total

    def pack_rest(target, carry):
        for k in range(group):
            rest_out[target, k] = packed([
                jnp.concatenate(
                    [staged[m, target * group + k, :, pl.ds(full, rest)],
                     jnp.zeros((rows, LANES - rest), jnp.float32)], axis=1)
                for m in range(local)
            ])
        return carry

    ahead = min(2, group)
    start_main(0)

    @pl.when(jnp.logical_not(has_low))
    def _():
        zero_edges(True)

    @pl.when(jnp.logical_not(has_high))
    def _():
        zero_edges(False)

    stage.wait()
    lax.fori_loop(0, ens_n, pack_rest, 0)
    rests[me] = rest_out[me]
    for shift in range(1, ens_n):
        f_rest(shift).start()

    def upper(size):
        return lax.broadcasted_iota(jnp.int32, (rows, size), 0) < half

    def turn(tile):
        return pltpu.roll(tile, half, 0)

    def neighbour_copies(source, targets, send, recv):
        return (
            pltpu.make_async_remote_copy(
                src_ref=source[0], dst_ref=targets[1], send_sem=send.at[0], recv_sem=recv.at[1],
                device_id={"lat": lat - 1}, device_id_type=MESH,
            ),
            pltpu.make_async_remote_copy(
                src_ref=source[1], dst_ref=targets[0], send_sem=send.at[1], recv_sem=recv.at[0],
                device_id={"lat": lat + 1}, device_id_type=MESH,
            ),
        )

    def start_both(copies):
        @pl.when(has_low)
        def _():
            copies[0].start()

        @pl.when(has_high)
        def _():
            copies[1].start()

    def recv_both(copies):
        @pl.when(has_low)
        def _():
            copies[1].wait_recv()

        @pl.when(has_high)
        def _():
            copies[0].wait_recv()

    def sent_both(copies):
        @pl.when(has_low)
        def _():
            copies[0].wait_send()

        @pl.when(has_high)
        def _():
            copies[1].wait_send()

    def lanes(h):
        return pl.ds(ranges[h][0], ranges[h][1] - ranges[h][0])

    def halo_copies(k, h):
        return neighbour_copies(
            (halo_out.at[k, 0, :, :, lanes(h)], halo_out.at[k, 1, :, :, lanes(h)]),
            (fields.at[k, pl.ds(members, pairs), :, lanes(h)],
             fields.at[k, pl.ds(members + pairs, pairs), :, lanes(h)]),
            h_send.at[k, h], h_recv.at[k, h],
        )

    def edge_copies(k, h):
        return neighbour_copies(
            (edge_out.at[k, 0, :, :, lanes(h)], edge_out.at[k, 1, :, :, lanes(h)]),
            (edge_in.at[k, 0, :, :, lanes(h)], edge_in.at[k, 1, :, :, lanes(h)]),
            e_send.at[k, h], e_recv.at[k, h],
        )

    for load in loads:
        load.wait()
    couples = group // 2
    obs_copies = neighbour_copies(
        (obs_halo.at[0], obs_halo.at[1]),
        (obs_fields.at[pl.ds(group, couples)], obs_fields.at[pl.ds(group + couples, couples)]),
        oh_send, oh_recv,
    )
    for c in range(group):
        obs_fields[c, :, pl.ds(full, LANES)] = jnp.zeros((rows, LANES), jnp.float32)
        obs_fields[c, :, pl.ds(0, width)] = obs_ref[c]
    for p in range(couples):
        one, two = obs_fields[p], obs_fields[p + couples]
        obs_halo[0, p] = jnp.where(upper(padded), one, turn(two))
        obs_halo[1, p] = jnp.where(upper(padded), turn(one), two)
    start_both(obs_copies)
    recv_both(obs_copies)
    values = obs_fields[...].reshape(2 * group * rows, padded)
    obs_sm[...] = split_dot(obs_band_ref[...], values, 3).reshape(2 * group, rows, padded)
    lon_blur(obs_sm, group, width)
    for k in range(1, ahead):
        start_main(k)

    def take_fields(k):
        f_own(k).wait()
        for h in range(len(ranges)):
            for shift in range(1, ens_n):
                f_main(k, h, shift).wait_recv()

            if h == last:
                def unpack(source, carry):
                    tile = rests[source, k]
                    for m in range(local):
                        fields[k, source * local + m, :, pl.ds(full, LANES)] = (
                            pltpu.roll(tile, LANES - m * rest, 1) if m else tile
                        )
                    return carry

                lax.fori_loop(0, ens_n, unpack, 0, unroll=True)

            def pack_halo(p, carry):
                one, two = fields[k, p, :, lanes(h)], fields[k, p + pairs, :, lanes(h)]
                mask = upper(one.shape[1])
                halo_out[k, 0, p, :, lanes(h)] = jnp.where(mask, one, turn(two))
                halo_out[k, 1, p, :, lanes(h)] = jnp.where(mask, turn(one), two)
                return carry

            lax.fori_loop(0, pairs, pack_halo, 0, unroll=4 if pairs % 4 == 0 else 1)
            start_both(halo_copies(k, h))

        @pl.when(k + ahead < group)
        def _():
            start_main(k + ahead)


    def forward(k):
        def smooth_block(b, carry):
            at = pl.ds(pl.multiple_of(b * block, block), block)
            values = fields[k, :, :, at].reshape(total_rows, block)
            smooth[:, :, at] = split_dot(band_ref[...], values, 3).reshape(2 * members, rows, block)
            return carry

        for h, (low, high) in enumerate(ranges):
            recv_both(halo_copies(k, h))
            lax.fori_loop(low // block, high // block, smooth_block, 0, unroll=True)
        lon_blur(smooth, members, width)

    def interact(k):
        weight = factor_ref[me * group + k] * jnp.broadcast_to(weight_ref[:, :1], (rows, LANES))
        pull = 0.95 / (members - 1)
        tiles = padded // LANES

        def couple(i, carry):
            scale, t = i // tiles, i % tiles
            at = pl.ds(pl.multiple_of(t * LANES, LANES), LANES)
            base = scale * members
            held = [smooth[base + m, :, at] for m in range(members)]
            sums = [None] * members
            for m in range(members):
                for other in range(m):
                    force = slope(held[m] - held[other])
                    sums[m] = force if sums[m] is None else sums[m] + force
                    sums[other] = -force if sums[other] is None else sums[other] - force
            analysis = obs_sm[scale * group + k, :, at]
            for m in range(members):
                smooth[base + m, :, at] = weight * (slope(held[m] - analysis) - pull * sums[m])
            return carry

        lax.fori_loop(0, 2 * tiles, couple, 0)

    def backward(k):
        lon_blur(smooth, members, width)

        def back_block(b, carry):
            at = pl.ds(pl.multiple_of(b * block, block), block)
            values = smooth[:, :, at].reshape(total_rows, block)
            out = split_dot(back_ref[...], values, 2).reshape(2 * members, rows, block)
            result[k, :, :, at] = out[:members]
            edge_out[k, 0, :, :, at] = out[members : members + pairs]
            edge_out[k, 1, :, :, at] = out[members + pairs :]
            return carry

        for h, (low, high) in enumerate(ranges):
            lax.fori_loop(low // block, high // block, back_block, 0, unroll=True)
            start_both(edge_copies(k, h))

    def b_main(k, h, shift):
        target = peer(shift)
        return pltpu.make_async_remote_copy(
            src_ref=result.at[k, pl.ds(target * local, local), :, sent_lanes(h)],
            dst_ref=main_ref.at[:, me * group + k, :, sent_lanes(h)],
            send_sem=b_send.at[k, h, shift], recv_sem=b_recv.at[k, h, shift],
            device_id={"ens": target}, device_id_type=MESH,
        )

    def b_rest(shift):
        target = peer(shift)
        return pltpu.make_async_remote_copy(
            src_ref=result_rest.at[target], dst_ref=rest_ref.at[pl.ds(me * group, group)],
            send_sem=br_send.at[shift], recv_sem=br_recv.at[shift],
            device_id={"ens": target}, device_id_type=MESH,
        )

    def b_own(k):
        return pltpu.make_async_copy(
            result.at[k, pl.ds(me * local, local), :, pl.ds(0, full)],
            main_ref.at[:, me * group + k, :, pl.ds(0, full)], bown_sem.at[k],
        )

    def write(k, source):
        channel = source * group + k
        return pltpu.make_async_copy(
            main_ref.at[:, channel], out_ref.at[:, channel], out_sem.at[k, source]
        )

    def finish(k):
        for h in range(len(ranges)):
            recv_both(edge_copies(k, h))

            def add(p, carry):
                low, high = edge_in[k, 0, p, :, lanes(h)], edge_in[k, 1, p, :, lanes(h)]
                mask = upper(low.shape[1])
                one, two = result[k, p, :, lanes(h)], result[k, p + pairs, :, lanes(h)]
                result[k, p, :, lanes(h)] = one + jnp.where(mask, low, turn(high))
                result[k, p + pairs, :, lanes(h)] = two + jnp.where(mask, turn(low), high)
                return carry

            lax.fori_loop(0, pairs, add, 0, unroll=4 if pairs % 4 == 0 else 1)
            for shift in range(1, ens_n):
                b_main(k, h, shift).start()

        def pack(target, carry):
            result_rest[target, k] = packed(
                [result[k, target * local + m, :, pl.ds(full, LANES)] for m in range(local)]
            )
            return carry

        lax.fori_loop(0, ens_n, pack, 0, unroll=True)
        b_own(k).start()

    for shift in range(1, ens_n):
        f_rest(shift).wait_recv()
    take_fields(0)

    def turn_of(k, carry):
        forward(k)

        @pl.when(k + 1 < group)
        def _():
            take_fields(k + 1)

        interact(k)

        @pl.when(k > 0)
        def _():
            finish(k - 1)

        backward(k)

        return carry

    lax.fori_loop(0, group, turn_of, 0)
    finish(group - 1)
    for shift in range(1, ens_n):
        b_rest(shift).start()
    rest_ref[pl.ds(me * group, group)] = result_rest[me]

    sent_both(obs_copies)

    def drain(k, carry):
        for h in range(len(ranges)):
            for shift in range(1, ens_n):
                f_main(k, h, shift).wait_send()
            sent_both(halo_copies(k, h))
            sent_both(edge_copies(k, h))
        return carry

    lax.fori_loop(0, group, drain, 0)
    for shift in range(1, ens_n):
        f_rest(shift).wait_send()
        b_rest(shift).wait()

    def collect(k, carry):
        for h in range(len(ranges)):
            for shift in range(1, ens_n):
                b_main(k, h, shift).wait()
        b_own(k).wait()

        def unpack(source, inner):
            channel = source * group + k
            tile = rest_ref[channel]
            for m in range(local):
                main_ref[m, channel, :, pl.ds(full, rest)] = tile[:, m * rest : (m + 1) * rest]
            write(k, source).start()
            return inner

        lax.fori_loop(0, ens_n, unpack, 0, unroll=True)
        return carry

    lax.fori_loop(0, group, collect, 0)

    def close(k, carry):
        for source in range(ens_n):
            write(k, source).wait()
        return carry

    lax.fori_loop(0, group, close, 0)


def pass_on(in_ref, out_ref, held, in_sem, out_sem):
    local, channels = in_ref.shape[:2]
    size = channels // COPIES
    parts = [(m, pl.ds(part * size, size)) for m in range(local) for part in range(COPIES)]
    reads = [pltpu.make_async_copy(in_ref.at[at], held.at[at], in_sem.at[i]) for i, at in enumerate(parts)]
    writes = [pltpu.make_async_copy(held.at[at], out_ref.at[at], out_sem.at[i]) for i, at in enumerate(parts)]
    for read in reads:
        read.start()
    for read, write in zip(reads, writes):
        read.wait()
        write.start()
    for write in writes:
        write.wait()


def body(prediction_array, verifying_analysis, variable_penalty_factor):
    local, channels, rows, width = prediction_array.shape
    group = verifying_analysis.shape[0]
    ens_n, lat_n = lax.axis_size("ens"), lax.axis_size("lat")
    members = local * ens_n
    pairs = members // 2
    full = width // LANES * LANES
    rest = width - full
    padded = full + LANES
    assert rows % 8 == 0 and rows // 2 >= COARSE and local * rest <= LANES and channels == group * ens_n
    assert members % 2 == 0 and group % 2 == 0 and LANES - rest >= 4 * COARSE

    bands = band_matrices(members, rows)
    band = jnp.asarray(bands, jnp.bfloat16)
    back = jnp.asarray(bands.transpose(0, 2, 1), jnp.bfloat16)
    square = bands.shape[1]
    obs_bands = band_matrices(group, rows)
    obs_band = jnp.asarray(np.concatenate([obs_bands] * 3, axis=2), jnp.bfloat16)
    ids = np.arange(lat_n * rows).astype(np.float32)
    degrees = np.float32(0.25) * (ids - np.float32((lat_n * rows - 1) / 2.0))
    weights = np.cos(degrees * np.float32(np.pi / 180.0)).astype(np.float32).reshape(lat_n, rows, 1)
    weights = jnp.asarray(np.pad(weights, ((0, 0), (0, 0), (0, LANES - 1))))

    dims = (ens_n, lat_n, local, members, group, rows, width)
    hbm = pl.BlockSpec(memory_space=pltpu.HBM)
    f32 = jnp.float32
    dma = pltpu.SemaphoreType.DMA
    cells = group * padded * rows
    gathered = pl.pallas_call(
        functools.partial(kernel, dims),
        out_shape=jax.ShapeDtypeStruct((local, channels, rows, width), f32),
        in_specs=[hbm, hbm, pl.BlockSpec(memory_space=pltpu.SMEM), hbm, hbm, hbm, hbm],
        out_specs=pl.BlockSpec(memory_space=pl.ANY),
        scratch_shapes=[
            pltpu.VMEM((local, channels, rows, width), f32),
            pltpu.VMEM((channels, rows, LANES), f32),
            pltpu.VMEM(verifying_analysis.shape, f32),
            pltpu.VMEM(weights.shape[1:], f32),
            pltpu.VMEM((square, 3 * square), jnp.bfloat16),
            pltpu.VMEM((square, 2 * square), jnp.bfloat16),
            pltpu.VMEM(obs_band.shape[1:], jnp.bfloat16),
            pltpu.VMEM((local, channels, rows, width), f32),
            pltpu.VMEM((group, members + 2 * pairs, rows, padded), f32),
            pltpu.VMEM((ens_n, group, rows, LANES), f32),
            pltpu.VMEM((ens_n, group, rows, LANES), f32),
            pltpu.VMEM((group, 2, pairs, rows, padded), f32),
            pltpu.VMEM((2 * group, rows, padded), f32),
            pltpu.VMEM((2, group // 2, rows, padded), f32),
            pltpu.VMEM((2 * group, rows, padded), f32),
            pltpu.VMEM((2 * members, rows, padded), f32),
            pltpu.VMEM((group, members, rows, padded), f32),
            pltpu.VMEM((ens_n, group, rows, LANES), f32),
            pltpu.VMEM((group, 2, pairs, rows, padded), f32),
            pltpu.VMEM((group, 2, pairs, rows, padded), f32),
            dma((group, 2, ens_n)), dma((group, 2, ens_n)), dma((ens_n,)), dma((ens_n,)),
            dma((group,)), dma,
            dma((group, 2, 2)), dma((group, 2, 2)), dma((2,)), dma((2,)), dma((group, 2, 2)), dma((group, 2, 2)),
            dma((group, 2, ens_n)), dma((group, 2, ens_n)), dma((ens_n,)), dma((ens_n,)),
            dma((group,)), dma((8,)), dma((group, ens_n)),
        ],
        compiler_params=pltpu.CompilerParams(
            collective_id=0, has_side_effects=True, vmem_limit_bytes=GRANT
        ),
        cost_estimate=pl.CostEstimate(
            flops=cells * members * members * 6, bytes_accessed=cells * members * 8,
            transcendentals=cells * members * members,
        ),
    )(prediction_array, verifying_analysis, variable_penalty_factor, weights, band, back, obs_band)
    return pl.pallas_call(
        pass_on,
        out_shape=jax.ShapeDtypeStruct(gathered.shape, f32),
        in_specs=[hbm],
        out_specs=hbm,
        scratch_shapes=[pltpu.VMEM(gathered.shape, f32), dma((local * COPIES,)), dma((local * COPIES,))],
        compiler_params=pltpu.CompilerParams(vmem_limit_bytes=GRANT),
    )(gathered)


def solution(mesh):
    placed = (P("ens", None, "lat", None), P("ens", "lat", None), P())
    return jax.shard_map(
        body, mesh=mesh, in_specs=placed, out_specs=P("ens", None, "lat", None), check_vma=False
    )
```

```python
import functools
import math

import jax
import jax.numpy as jnp
import numpy as np
from jax import lax
from jax.experimental import pallas as pl
from jax.experimental.pallas import tpu as pltpu
from jax.sharding import PartitionSpec as P

COARSE = 3
LANES = 128
COPIES = 4
GRANT = 62 * 1024 * 1024
MESH = pl.DeviceIdType.MESH


def round_up(value, unit):
    return -(-value // unit) * unit


def band_matrices(fields, rows):
    half = rows // 2
    pairs = fields // 2
    out = np.zeros((4, 2 * fields * rows, 2 * fields * rows), np.float32)
    window = 2 * rows
    band = 0.5 * np.eye(window) + 0.25 * np.eye(window, k=1) + 0.25 * np.eye(window, k=-1)
    places = np.arange(window) - half
    for variant in range(4):
        keep = np.ones(window)
        if variant & 1:
            keep[places < 0] = 0.0
        if variant & 2:
            keep[places >= rows] = 0.0
        step = keep[:, None] * band * keep[None, :]
        scales = (step, np.linalg.matrix_power(step, COARSE))
        for scale, matrix in enumerate(scales):
            matrix = matrix[half : half + rows]
            for field in range(fields):
                at = (scale * fields + field) * rows
                out[variant, at : at + rows, field * rows : (field + 1) * rows] = matrix[:, half : half + rows]
                tile, part = field % pairs, field // pairs
                low = (fields + tile) * rows + part * half
                out[variant, at : at + rows, low : low + half] = matrix[:, :half]
                high = (fields + pairs + tile) * rows + part * half
                out[variant, at : at + rows, high : high + half] = matrix[:, half + rows :]
    return out


def split_dot(matrix, values, parts):
    pieces = []
    for _ in range(parts):
        piece = values.astype(jnp.bfloat16)
        pieces.append(piece)
        values = values - piece.astype(jnp.float32)
    return jnp.dot(matrix, jnp.concatenate(pieces, axis=0), preferred_element_type=jnp.float32)


def wrapped(tiles, width):
    whole = width // LANES
    rest = width - whole * LANES
    last = tiles[:, whole * LANES :]
    lane = lax.broadcasted_iota(jnp.int32, last.shape, 1)
    ahead = pltpu.roll(tiles[:, :LANES], rest, 1)
    behind = pltpu.roll(last, LANES - rest, 1)
    last = jnp.where(lane < rest, last, jnp.where(lane < (LANES + rest) // 2, ahead, behind))
    return jnp.concatenate([tiles[:, : whole * LANES], last], axis=1)


def lon_pass(tiles, passes):
    size = tiles.shape[1]
    total = math.comb(2 * passes, passes) / 4.0**passes * tiles
    for far in range(1, passes + 1):
        both = pltpu.roll(tiles, far, 1) + pltpu.roll(tiles, size - far, 1)
        total = total + math.comb(2 * passes, passes + far) / 4.0**passes * both
    return total


def lon_blur(ref, count, width):
    def step(field, carry):
        ref[field] = lon_pass(wrapped(ref[field], width), 1)
        ref[count + field] = lon_pass(wrapped(ref[count + field], width), COARSE)
        return carry

    lax.fori_loop(0, count, step, 0, unroll=4 if count % 4 == 0 else 2)


def slope(differ):
    return differ * lax.rsqrt(differ * differ + 0.01)


def kernel(
    dims,
    in_ref, obs_hbm, factor_ref, weight_hbm, band_hbm, back_hbm, obs_band_hbm,
    out_ref,
    main_ref, rest_ref, obs_ref, weight_ref, band_ref, back_ref, obs_band_ref,
    staged, fields, rests, rest_out, halo_out, obs_fields, obs_halo, obs_sm, smooth, result, result_rest,
    edge_out, edge_in,
    f_send, f_recv, fr_send, fr_recv, own_sem, stage_sem,
    h_send, h_recv, oh_send, oh_recv, e_send, e_recv,
    b_send, b_recv, br_send, br_recv, bown_sem, load_sem, out_sem,
):
    ens_n, lat_n, local, members, group, rows, width = dims
    half = rows // 2
    pairs = members // 2
    full = width // LANES * LANES
    rest = width - full
    padded = full + LANES
    total_rows = 2 * members * rows
    block = 2 * LANES if padded % (2 * LANES) == 0 else LANES
    cut = (padded // block + 1) // 2 * block
    ranges = ((0, cut), (cut, padded))
    last = len(ranges) - 1
    me = lax.axis_index("ens")
    lat = lax.axis_index("lat")
    has_low = lat > 0
    has_high = lat < lat_n - 1
    variant = (lat == 0).astype(jnp.int32) + 2 * (lat == lat_n - 1).astype(jnp.int32)

    def peer(shift):
        return lax.rem(me + shift, ens_n)

    barrier = pltpu.get_barrier_semaphore()
    for shift in range(1, ens_n):
        pl.semaphore_signal(barrier, inc=1, device_id={"ens": peer(shift)}, device_id_type=MESH)

    @pl.when(has_low)
    def _():
        pl.semaphore_signal(barrier, inc=1, device_id={"lat": lat - 1}, device_id_type=MESH)

    @pl.when(has_high)
    def _():
        pl.semaphore_signal(barrier, inc=1, device_id={"lat": lat + 1}, device_id_type=MESH)

    stage = pltpu.make_async_copy(in_ref, staged, stage_sem)
    stage.start()
    loads = [
        pltpu.make_async_copy(source, target, load_sem.at[i])
        for i, (source, target) in enumerate((
            (obs_hbm, obs_ref),
            (weight_hbm.at[lat], weight_ref),
            *((band_hbm.at[variant], band_ref.at[:, pl.ds(part * total_rows, total_rows)]) for part in range(3)),
            *((back_hbm.at[variant], back_ref.at[:, pl.ds(part * total_rows, total_rows)]) for part in range(2)),
            (obs_band_hbm.at[variant], obs_band_ref),
        ))
    ]
    for load in loads:
        load.start()

    def zero_edges(low):
        at = members if low else members + pairs
        side = 0 if low else 1

        def clear(k, carry):
            def tile(p, inner):
                fields[k, at + p] = jnp.zeros((rows, padded), jnp.float32)
                edge_in[k, side, p] = jnp.zeros((rows, padded), jnp.float32)
                return inner

            lax.fori_loop(0, pairs, tile, 0)
            return carry

        lax.fori_loop(0, group, clear, 0)
        obs_at = group if low else group + group // 2
        for p in range(group // 2):
            obs_fields[obs_at + p] = jnp.zeros((rows, padded), jnp.float32)

    pl.semaphore_wait(barrier, ens_n - 1 + has_low.astype(jnp.int32) + has_high.astype(jnp.int32))

    def sent_lanes(h):
        low, high = ranges[h]
        return pl.ds(low, min(high, full) - low)

    def f_main(k, h, shift):
        target = peer(shift)
        return pltpu.make_async_remote_copy(
            src_ref=in_ref.at[:, target * group + k, :, sent_lanes(h)],
            dst_ref=fields.at[k, pl.ds(me * local, local), :, sent_lanes(h)],
            send_sem=f_send.at[k, h, shift], recv_sem=f_recv.at[k, h, shift],
            device_id={"ens": target}, device_id_type=MESH,
        )

    def f_rest(shift):
        target = peer(shift)
        return pltpu.make_async_remote_copy(
            src_ref=rest_out.at[target], dst_ref=rests.at[me],
            send_sem=fr_send.at[shift], recv_sem=fr_recv.at[shift],
            device_id={"ens": target}, device_id_type=MESH,
        )

    def f_own(k):
        return pltpu.make_async_copy(
            in_ref.at[:, me * group + k, :, pl.ds(0, full)],
            fields.at[k, pl.ds(me * local, local), :, pl.ds(0, full)],
            own_sem.at[k],
        )

    def start_main(k):
        for h in range(len(ranges)):
            for shift in range(1, ens_n):
                f_main(k, h, shift).start()
        f_own(k).start()

    lane = lax.broadcasted_iota(jnp.int32, (rows, LANES), 1)

    def packed(tiles):
        total = tiles[0]
        for m in range(1, local):
            total = jnp.where(lane < m * rest, total, pltpu.roll(tiles[m], m * rest, 1))
        return total

    def pack_rest(target, carry):
        for k in range(group):
            rest_out[target, k] = packed([
                jnp.concatenate(
                    [staged[m, target * group + k, :, pl.ds(full, rest)],
                     jnp.zeros((rows, LANES - rest), jnp.float32)], axis=1)
                for m in range(local)
            ])
        return carry

    start_main(0)

    @pl.when(jnp.logical_not(has_low))
    def _():
        zero_edges(True)

    @pl.when(jnp.logical_not(has_high))
    def _():
        zero_edges(False)

    stage.wait()
    lax.fori_loop(0, ens_n, pack_rest, 0)
    rests[me] = rest_out[me]
    for shift in range(1, ens_n):
        f_rest(shift).start()

    def upper(size):
        return lax.broadcasted_iota(jnp.int32, (rows, size), 0) < half

    def turn(tile):
        return pltpu.roll(tile, half, 0)

    def neighbour_copies(source, targets, send, recv):
        return (
            pltpu.make_async_remote_copy(
                src_ref=source[0], dst_ref=targets[1], send_sem=send.at[0], recv_sem=recv.at[1],
                device_id={"lat": lat - 1}, device_id_type=MESH,
            ),
            pltpu.make_async_remote_copy(
                src_ref=source[1], dst_ref=targets[0], send_sem=send.at[1], recv_sem=recv.at[0],
                device_id={"lat": lat + 1}, device_id_type=MESH,
            ),
        )

    def start_both(copies):
        @pl.when(has_low)
        def _():
            copies[0].start()

        @pl.when(has_high)
        def _():
            copies[1].start()

    def recv_both(copies):
        @pl.when(has_low)
        def _():
            copies[1].wait_recv()

        @pl.when(has_high)
        def _():
            copies[0].wait_recv()

    def sent_both(copies):
        @pl.when(has_low)
        def _():
            copies[0].wait_send()

        @pl.when(has_high)
        def _():
            copies[1].wait_send()

    def lanes(h):
        return pl.ds(ranges[h][0], ranges[h][1] - ranges[h][0])

    def halo_copies(k, h):
        return neighbour_copies(
            (halo_out.at[k, 0, :, :, lanes(h)], halo_out.at[k, 1, :, :, lanes(h)]),
            (fields.at[k, pl.ds(members, pairs), :, lanes(h)],
             fields.at[k, pl.ds(members + pairs, pairs), :, lanes(h)]),
            h_send.at[k, h], h_recv.at[k, h],
        )

    def edge_copies(k, h):
        return neighbour_copies(
            (edge_out.at[k, 0, :, :, lanes(h)], edge_out.at[k, 1, :, :, lanes(h)]),
            (edge_in.at[k, 0, :, :, lanes(h)], edge_in.at[k, 1, :, :, lanes(h)]),
            e_send.at[k, h], e_recv.at[k, h],
        )

    for load in loads:
        load.wait()
    couples = group // 2
    obs_copies = neighbour_copies(
        (obs_halo.at[0], obs_halo.at[1]),
        (obs_fields.at[pl.ds(group, couples)], obs_fields.at[pl.ds(group + couples, couples)]),
        oh_send, oh_recv,
    )
    for c in range(group):
        obs_fields[c, :, pl.ds(full, LANES)] = jnp.zeros((rows, LANES), jnp.float32)
        obs_fields[c, :, pl.ds(0, width)] = obs_ref[c]
    for p in range(couples):
        one, two = obs_fields[p], obs_fields[p + couples]
        obs_halo[0, p] = jnp.where(upper(padded), one, turn(two))
        obs_halo[1, p] = jnp.where(upper(padded), turn(one), two)
    start_both(obs_copies)
    recv_both(obs_copies)
    values = obs_fields[...].reshape(2 * group * rows, padded)
    obs_sm[...] = split_dot(obs_band_ref[...], values, 3).reshape(2 * group, rows, padded)
    lon_blur(obs_sm, group, width)

    def take_fields(k):
        f_own(k).wait()
        for h in range(len(ranges)):
            for shift in range(1, ens_n):
                f_main(k, h, shift).wait_recv()

            if h == last:
                @pl.when(k + 1 < group)
                def _():
                    start_main(k + 1)

                def unpack(source, carry):
                    tile = rests[source, k]
                    for m in range(local):
                        fields[k, source * local + m, :, pl.ds(full, LANES)] = (
                            pltpu.roll(tile, LANES - m * rest, 1) if m else tile
                        )
                    return carry

                lax.fori_loop(0, ens_n, unpack, 0, unroll=True)

            def pack_halo(p, carry):
                one, two = fields[k, p, :, lanes(h)], fields[k, p + pairs, :, lanes(h)]
                mask = upper(one.shape[1])
                halo_out[k, 0, p, :, lanes(h)] = jnp.where(mask, one, turn(two))
                halo_out[k, 1, p, :, lanes(h)] = jnp.where(mask, turn(one), two)
                return carry

            lax.fori_loop(0, pairs, pack_halo, 0, unroll=4 if pairs % 4 == 0 else 1)
            start_both(halo_copies(k, h))

    def forward(k):
        def smooth_block(b, carry):
            at = pl.ds(pl.multiple_of(b * block, block), block)
            values = fields[k, :, :, at].reshape(total_rows, block)
            smooth[:, :, at] = split_dot(band_ref[...], values, 3).reshape(2 * members, rows, block)
            return carry

        for h, (low, high) in enumerate(ranges):
            recv_both(halo_copies(k, h))
            lax.fori_loop(low // block, high // block, smooth_block, 0, unroll=True)
        lon_blur(smooth, members, width)

    def interact(k):
        weight = factor_ref[me * group + k] * jnp.broadcast_to(weight_ref[:, :1], (rows, LANES))
        pull = 0.95 / (members - 1)
        tiles = padded // LANES

        def couple(i, carry):
            scale, t = i // tiles, i % tiles
            at = pl.ds(pl.multiple_of(t * LANES, LANES), LANES)
            base = scale * members
            held = [smooth[base + m, :, at] for m in range(members)]
            sums = [None] * members
            for m in range(members):
                for other in range(m):
                    force = slope(held[m] - held[other])
                    sums[m] = force if sums[m] is None else sums[m] + force
                    sums[other] = -force if sums[other] is None else sums[other] - force
            analysis = obs_sm[scale * group + k, :, at]
            for m in range(members):
                smooth[base + m, :, at] = weight * (slope(held[m] - analysis) - pull * sums[m])
            return carry

        lax.fori_loop(0, 2 * tiles, couple, 0)

    def backward(k):
        lon_blur(smooth, members, width)

        def back_block(b, carry):
            at = pl.ds(pl.multiple_of(b * block, block), block)
            values = smooth[:, :, at].reshape(total_rows, block)
            out = split_dot(back_ref[...], values, 2).reshape(2 * members, rows, block)
            result[k, :, :, at] = out[:members]
            edge_out[k, 0, :, :, at] = out[members : members + pairs]
            edge_out[k, 1, :, :, at] = out[members + pairs :]
            return carry

        for h, (low, high) in enumerate(ranges):
            lax.fori_loop(low // block, high // block, back_block, 0, unroll=True)
            start_both(edge_copies(k, h))

    def b_main(k, h, shift):
        target = peer(shift)
        return pltpu.make_async_remote_copy(
            src_ref=result.at[k, pl.ds(target * local, local), :, sent_lanes(h)],
            dst_ref=main_ref.at[:, me * group + k, :, sent_lanes(h)],
            send_sem=b_send.at[k, h, shift], recv_sem=b_recv.at[k, h, shift],
            device_id={"ens": target}, device_id_type=MESH,
        )

    def b_rest(shift):
        target = peer(shift)
        return pltpu.make_async_remote_copy(
            src_ref=result_rest.at[target], dst_ref=rest_ref.at[pl.ds(me * group, group)],
            send_sem=br_send.at[shift], recv_sem=br_recv.at[shift],
            device_id={"ens": target}, device_id_type=MESH,
        )

    def b_own(k):
        return pltpu.make_async_copy(
            result.at[k, pl.ds(me * local, local), :, pl.ds(0, full)],
            main_ref.at[:, me * group + k, :, pl.ds(0, full)], bown_sem.at[k],
        )

    def write(k, source):
        channel = source * group + k
        return pltpu.make_async_copy(
            main_ref.at[:, channel], out_ref.at[:, channel], out_sem.at[k, source]
        )

    def finish(k):
        for h in range(len(ranges)):
            recv_both(edge_copies(k, h))

            def add(p, carry):
                low, high = edge_in[k, 0, p, :, lanes(h)], edge_in[k, 1, p, :, lanes(h)]
                mask = upper(low.shape[1])
                one, two = result[k, p, :, lanes(h)], result[k, p + pairs, :, lanes(h)]
                result[k, p, :, lanes(h)] = one + jnp.where(mask, low, turn(high))
                result[k, p + pairs, :, lanes(h)] = two + jnp.where(mask, turn(low), high)
                return carry

            lax.fori_loop(0, pairs, add, 0, unroll=4 if pairs % 4 == 0 else 1)
            for shift in range(1, ens_n):
                b_main(k, h, shift).start()

        def pack(target, carry):
            result_rest[target, k] = packed(
                [result[k, target * local + m, :, pl.ds(full, LANES)] for m in range(local)]
            )
            return carry

        lax.fori_loop(0, ens_n, pack, 0, unroll=True)
        b_own(k).start()

    for shift in range(1, ens_n):
        f_rest(shift).wait_recv()
    take_fields(0)

    def turn_of(k, carry):
        forward(k)

        @pl.when(k + 1 < group)
        def _():
            take_fields(k + 1)

        interact(k)

        @pl.when(k > 0)
        def _():
            finish(k - 1)

        backward(k)

        return carry

    lax.fori_loop(0, group, turn_of, 0)
    finish(group - 1)
    for shift in range(1, ens_n):
        b_rest(shift).start()
    rest_ref[pl.ds(me * group, group)] = result_rest[me]

    sent_both(obs_copies)

    def drain(k, carry):
        for h in range(len(ranges)):
            for shift in range(1, ens_n):
                f_main(k, h, shift).wait_send()
            sent_both(halo_copies(k, h))
            sent_both(edge_copies(k, h))
        return carry

    lax.fori_loop(0, group, drain, 0)
    for shift in range(1, ens_n):
        f_rest(shift).wait_send()
        b_rest(shift).wait()

    def collect(k, carry):
        for h in range(len(ranges)):
            for shift in range(1, ens_n):
                b_main(k, h, shift).wait()
        b_own(k).wait()

        def unpack(source, inner):
            channel = source * group + k
            tile = rest_ref[channel]
            for m in range(local):
                main_ref[m, channel, :, pl.ds(full, rest)] = tile[:, m * rest : (m + 1) * rest]
            write(k, source).start()
            return inner

        lax.fori_loop(0, ens_n, unpack, 0, unroll=True)
        return carry

    lax.fori_loop(0, group, collect, 0)

    def close(k, carry):
        for source in range(ens_n):
            write(k, source).wait()
        return carry

    lax.fori_loop(0, group, close, 0)


def pass_on(in_ref, out_ref, held, in_sem, out_sem):
    local, channels = in_ref.shape[:2]
    size = channels // COPIES
    parts = [(m, pl.ds(part * size, size)) for m in range(local) for part in range(COPIES)]
    reads = [pltpu.make_async_copy(in_ref.at[at], held.at[at], in_sem.at[i]) for i, at in enumerate(parts)]
    writes = [pltpu.make_async_copy(held.at[at], out_ref.at[at], out_sem.at[i]) for i, at in enumerate(parts)]
    for read in reads:
        read.start()
    for read, write in zip(reads, writes):
        read.wait()
        write.start()
    for write in writes:
        write.wait()


def body(prediction_array, verifying_analysis, variable_penalty_factor):
    local, channels, rows, width = prediction_array.shape
    group = verifying_analysis.shape[0]
    ens_n, lat_n = lax.axis_size("ens"), lax.axis_size("lat")
    members = local * ens_n
    pairs = members // 2
    full = width // LANES * LANES
    rest = width - full
    padded = full + LANES
    assert rows % 8 == 0 and rows // 2 >= COARSE and local * rest <= LANES and channels == group * ens_n
    assert members % 2 == 0 and group % 2 == 0 and LANES - rest >= 4 * COARSE

    bands = band_matrices(members, rows)
    band = jnp.asarray(bands, jnp.bfloat16)
    back = jnp.asarray(bands.transpose(0, 2, 1), jnp.bfloat16)
    square = bands.shape[1]
    obs_bands = band_matrices(group, rows)
    obs_band = jnp.asarray(np.concatenate([obs_bands] * 3, axis=2), jnp.bfloat16)
    ids = np.arange(lat_n * rows).astype(np.float32)
    degrees = np.float32(0.25) * (ids - np.float32((lat_n * rows - 1) / 2.0))
    weights = np.cos(degrees * np.float32(np.pi / 180.0)).astype(np.float32).reshape(lat_n, rows, 1)
    weights = jnp.asarray(np.pad(weights, ((0, 0), (0, 0), (0, LANES - 1))))

    dims = (ens_n, lat_n, local, members, group, rows, width)
    hbm = pl.BlockSpec(memory_space=pltpu.HBM)
    f32 = jnp.float32
    dma = pltpu.SemaphoreType.DMA
    cells = group * padded * rows
    gathered = pl.pallas_call(
        functools.partial(kernel, dims),
        out_shape=jax.ShapeDtypeStruct((local, channels, rows, width), f32),
        in_specs=[hbm, hbm, pl.BlockSpec(memory_space=pltpu.SMEM), hbm, hbm, hbm, hbm],
        out_specs=pl.BlockSpec(memory_space=pl.ANY),
        scratch_shapes=[
            pltpu.VMEM((local, channels, rows, width), f32),
            pltpu.VMEM((channels, rows, LANES), f32),
            pltpu.VMEM(verifying_analysis.shape, f32),
            pltpu.VMEM(weights.shape[1:], f32),
            pltpu.VMEM((square, 3 * square), jnp.bfloat16),
            pltpu.VMEM((square, 2 * square), jnp.bfloat16),
            pltpu.VMEM(obs_band.shape[1:], jnp.bfloat16),
            pltpu.VMEM((local, channels, rows, width), f32),
            pltpu.VMEM((group, members + 2 * pairs, rows, padded), f32),
            pltpu.VMEM((ens_n, group, rows, LANES), f32),
            pltpu.VMEM((ens_n, group, rows, LANES), f32),
            pltpu.VMEM((group, 2, pairs, rows, padded), f32),
            pltpu.VMEM((2 * group, rows, padded), f32),
            pltpu.VMEM((2, group // 2, rows, padded), f32),
            pltpu.VMEM((2 * group, rows, padded), f32),
            pltpu.VMEM((2 * members, rows, padded), f32),
            pltpu.VMEM((group, members, rows, padded), f32),
            pltpu.VMEM((ens_n, group, rows, LANES), f32),
            pltpu.VMEM((group, 2, pairs, rows, padded), f32),
            pltpu.VMEM((group, 2, pairs, rows, padded), f32),
            dma((group, 2, ens_n)), dma((group, 2, ens_n)), dma((ens_n,)), dma((ens_n,)),
            dma((group,)), dma,
            dma((group, 2, 2)), dma((group, 2, 2)), dma((2,)), dma((2,)), dma((group, 2, 2)), dma((group, 2, 2)),
            dma((group, 2, ens_n)), dma((group, 2, ens_n)), dma((ens_n,)), dma((ens_n,)),
            dma((group,)), dma((8,)), dma((group, ens_n)),
        ],
        compiler_params=pltpu.CompilerParams(
            collective_id=0, has_side_effects=True, vmem_limit_bytes=GRANT
        ),
        cost_estimate=pl.CostEstimate(
            flops=cells * members * members * 6, bytes_accessed=cells * members * 8,
            transcendentals=cells * members * members,
        ),
    )(prediction_array, verifying_analysis, variable_penalty_factor, weights, band, back, obs_band)
    return pl.pallas_call(
        pass_on,
        out_shape=jax.ShapeDtypeStruct(gathered.shape, f32),
        in_specs=[hbm],
        out_specs=hbm,
        scratch_shapes=[pltpu.VMEM(gathered.shape, f32), dma((local * COPIES,)), dma((local * COPIES,))],
        compiler_params=pltpu.CompilerParams(vmem_limit_bytes=GRANT),
    )(gathered)


def solution(mesh):
    placed = (P("ens", None, "lat", None), P("ens", "lat", None), P())
    return jax.shard_map(
        body, mesh=mesh, in_specs=placed, out_specs=P("ens", None, "lat", None), check_vma=False
    )
```

```python
import functools
import math

import jax
import jax.numpy as jnp
import numpy as np
from jax import lax
from jax.experimental import pallas as pl
from jax.experimental.pallas import tpu as pltpu
from jax.sharding import PartitionSpec as P

COARSE = 3
LANES = 128
COPIES = 4
GRANT = 62 * 1024 * 1024
MESH = pl.DeviceIdType.MESH


def round_up(value, unit):
    return -(-value // unit) * unit


def band_matrices(fields, rows):
    half = rows // 2
    pairs = fields // 2
    out = np.zeros((4, 2 * fields * rows, 2 * fields * rows), np.float32)
    window = 2 * rows
    band = 0.5 * np.eye(window) + 0.25 * np.eye(window, k=1) + 0.25 * np.eye(window, k=-1)
    places = np.arange(window) - half
    for variant in range(4):
        keep = np.ones(window)
        if variant & 1:
            keep[places < 0] = 0.0
        if variant & 2:
            keep[places >= rows] = 0.0
        step = keep[:, None] * band * keep[None, :]
        scales = (step, np.linalg.matrix_power(step, COARSE))
        for scale, matrix in enumerate(scales):
            matrix = matrix[half : half + rows]
            for field in range(fields):
                at = (scale * fields + field) * rows
                out[variant, at : at + rows, field * rows : (field + 1) * rows] = matrix[:, half : half + rows]
                tile, part = field % pairs, field // pairs
                low = (fields + tile) * rows + part * half
                out[variant, at : at + rows, low : low + half] = matrix[:, :half]
                high = (fields + pairs + tile) * rows + part * half
                out[variant, at : at + rows, high : high + half] = matrix[:, half + rows :]
    return out


def split_dot(matrix, values, parts):
    pieces = []
    for _ in range(parts):
        piece = values.astype(jnp.bfloat16)
        pieces.append(piece)
        values = values - piece.astype(jnp.float32)
    return jnp.dot(matrix, jnp.concatenate(pieces, axis=0), preferred_element_type=jnp.float32)


def wrapped(tiles, width):
    whole = width // LANES
    rest = width - whole * LANES
    last = tiles[:, whole * LANES :]
    lane = lax.broadcasted_iota(jnp.int32, last.shape, 1)
    ahead = pltpu.roll(tiles[:, :LANES], rest, 1)
    behind = pltpu.roll(last, LANES - rest, 1)
    last = jnp.where(lane < rest, last, jnp.where(lane < (LANES + rest) // 2, ahead, behind))
    return jnp.concatenate([tiles[:, : whole * LANES], last], axis=1)


def lon_pass(tiles, passes):
    size = tiles.shape[1]
    total = math.comb(2 * passes, passes) / 4.0**passes * tiles
    for far in range(1, passes + 1):
        both = pltpu.roll(tiles, far, 1) + pltpu.roll(tiles, size - far, 1)
        total = total + math.comb(2 * passes, passes + far) / 4.0**passes * both
    return total


def lon_blur(ref, count, width):
    def step(field, carry):
        ref[field] = lon_pass(wrapped(ref[field], width), 1)
        ref[count + field] = lon_pass(wrapped(ref[count + field], width), COARSE)
        return carry

    lax.fori_loop(0, count, step, 0, unroll=4 if count % 4 == 0 else 2)


def slope(differ):
    return differ * lax.rsqrt(differ * differ + 0.01)


def kernel(
    dims,
    in_ref, obs_hbm, factor_ref, weight_hbm, band_hbm, back_hbm, obs_band_hbm,
    out_ref,
    main_ref, rest_ref, obs_ref, weight_ref, band_ref, back_ref, obs_band_ref,
    staged, fields, rests, rest_out, halo_out, obs_fields, obs_halo, obs_sm, smooth, result, result_rest,
    edge_out, edge_in,
    f_send, f_recv, fr_send, fr_recv, own_sem, stage_sem,
    h_send, h_recv, oh_send, oh_recv, e_send, e_recv,
    b_send, b_recv, br_send, br_recv, bown_sem, load_sem, out_sem,
):
    ens_n, lat_n, local, members, group, rows, width = dims
    half = rows // 2
    pairs = members // 2
    full = width // LANES * LANES
    rest = width - full
    padded = full + LANES
    total_rows = 2 * members * rows
    block = 2 * LANES if padded % (2 * LANES) == 0 else LANES
    cut = (padded // block + 1) // 2 * block
    ranges = ((0, cut), (cut, padded))
    last = len(ranges) - 1
    me = lax.axis_index("ens")
    lat = lax.axis_index("lat")
    has_low = lat > 0
    has_high = lat < lat_n - 1
    variant = (lat == 0).astype(jnp.int32) + 2 * (lat == lat_n - 1).astype(jnp.int32)

    def peer(shift):
        return lax.rem(me + shift, ens_n)

    barrier = pltpu.get_barrier_semaphore()
    for shift in range(1, ens_n):
        pl.semaphore_signal(barrier, inc=1, device_id={"ens": peer(shift)}, device_id_type=MESH)

    @pl.when(has_low)
    def _():
        pl.semaphore_signal(barrier, inc=1, device_id={"lat": lat - 1}, device_id_type=MESH)

    @pl.when(has_high)
    def _():
        pl.semaphore_signal(barrier, inc=1, device_id={"lat": lat + 1}, device_id_type=MESH)

    stage = pltpu.make_async_copy(in_ref, staged, stage_sem)
    stage.start()
    loads = [
        pltpu.make_async_copy(source, target, load_sem.at[i])
        for i, (source, target) in enumerate((
            (obs_hbm, obs_ref),
            (weight_hbm.at[lat], weight_ref),
            *((band_hbm.at[variant], band_ref.at[:, pl.ds(part * total_rows, total_rows)]) for part in range(3)),
            *((back_hbm.at[variant], back_ref.at[:, pl.ds(part * total_rows, total_rows)]) for part in range(2)),
            (obs_band_hbm.at[variant], obs_band_ref),
        ))
    ]
    for load in loads:
        load.start()

    def zero_edges(low):
        at = members if low else members + pairs
        side = 0 if low else 1

        def clear(k, carry):
            def tile(p, inner):
                fields[k, at + p] = jnp.zeros((rows, padded), jnp.float32)
                edge_in[k, side, p] = jnp.zeros((rows, padded), jnp.float32)
                return inner

            lax.fori_loop(0, pairs, tile, 0)
            return carry

        lax.fori_loop(0, group, clear, 0)
        obs_at = group if low else group + group // 2
        for p in range(group // 2):
            obs_fields[obs_at + p] = jnp.zeros((rows, padded), jnp.float32)

    pl.semaphore_wait(barrier, ens_n - 1 + has_low.astype(jnp.int32) + has_high.astype(jnp.int32))

    def sent_lanes(h):
        low, high = ranges[h]
        return pl.ds(low, min(high, full) - low)

    def f_main(k, h, shift):
        target = peer(shift)
        return pltpu.make_async_remote_copy(
            src_ref=in_ref.at[:, target * group + k, :, sent_lanes(h)],
            dst_ref=fields.at[k, pl.ds(me * local, local), :, sent_lanes(h)],
            send_sem=f_send.at[k, h, shift], recv_sem=f_recv.at[k, h, shift],
            device_id={"ens": target}, device_id_type=MESH,
        )

    def f_rest(shift):
        target = peer(shift)
        return pltpu.make_async_remote_copy(
            src_ref=rest_out.at[target], dst_ref=rests.at[me],
            send_sem=fr_send.at[shift], recv_sem=fr_recv.at[shift],
            device_id={"ens": target}, device_id_type=MESH,
        )

    def f_own(k):
        return pltpu.make_async_copy(
            in_ref.at[:, me * group + k, :, pl.ds(0, full)],
            fields.at[k, pl.ds(me * local, local), :, pl.ds(0, full)],
            own_sem.at[k],
        )

    def start_main(k):
        for h in range(len(ranges)):
            for shift in range(1, ens_n):
                f_main(k, h, shift).start()
        f_own(k).start()

    lane = lax.broadcasted_iota(jnp.int32, (rows, LANES), 1)

    def packed(tiles):
        total = tiles[0]
        for m in range(1, local):
            total = jnp.where(lane < m * rest, total, pltpu.roll(tiles[m], m * rest, 1))
        return total

    def pack_rest(target, carry):
        for k in range(group):
            rest_out[target, k] = packed([
                jnp.concatenate(
                    [staged[m, target * group + k, :, pl.ds(full, rest)],
                     jnp.zeros((rows, LANES - rest), jnp.float32)], axis=1)
                for m in range(local)
            ])
        return carry

    start_main(0)

    @pl.when(jnp.logical_not(has_low))
    def _():
        zero_edges(True)

    @pl.when(jnp.logical_not(has_high))
    def _():
        zero_edges(False)

    stage.wait()
    lax.fori_loop(0, ens_n, pack_rest, 0)
    rests[me] = rest_out[me]
    for shift in range(1, ens_n):
        f_rest(shift).start()

    def upper(size):
        return lax.broadcasted_iota(jnp.int32, (rows, size), 0) < half

    def turn(tile):
        return pltpu.roll(tile, half, 0)

    def neighbour_copies(source, targets, send, recv):
        return (
            pltpu.make_async_remote_copy(
                src_ref=source[0], dst_ref=targets[1], send_sem=send.at[0], recv_sem=recv.at[1],
                device_id={"lat": lat - 1}, device_id_type=MESH,
            ),
            pltpu.make_async_remote_copy(
                src_ref=source[1], dst_ref=targets[0], send_sem=send.at[1], recv_sem=recv.at[0],
                device_id={"lat": lat + 1}, device_id_type=MESH,
            ),
        )

    def start_both(copies):
        @pl.when(has_low)
        def _():
            copies[0].start()

        @pl.when(has_high)
        def _():
            copies[1].start()

    def recv_both(copies):
        @pl.when(has_low)
        def _():
            copies[1].wait_recv()

        @pl.when(has_high)
        def _():
            copies[0].wait_recv()

    def sent_both(copies):
        @pl.when(has_low)
        def _():
            copies[0].wait_send()

        @pl.when(has_high)
        def _():
            copies[1].wait_send()

    def lanes(h):
        return pl.ds(ranges[h][0], ranges[h][1] - ranges[h][0])

    def halo_copies(k, h):
        return neighbour_copies(
            (halo_out.at[k, 0, :, :, lanes(h)], halo_out.at[k, 1, :, :, lanes(h)]),
            (fields.at[k, pl.ds(members, pairs), :, lanes(h)],
             fields.at[k, pl.ds(members + pairs, pairs), :, lanes(h)]),
            h_send.at[k, h], h_recv.at[k, h],
        )

    def edge_copies(k, h):
        return neighbour_copies(
            (edge_out.at[k, 0, :, :, lanes(h)], edge_out.at[k, 1, :, :, lanes(h)]),
            (edge_in.at[k, 0, :, :, lanes(h)], edge_in.at[k, 1, :, :, lanes(h)]),
            e_send.at[k, h], e_recv.at[k, h],
        )

    for load in loads:
        load.wait()
    couples = group // 2
    obs_copies = neighbour_copies(
        (obs_halo.at[0], obs_halo.at[1]),
        (obs_fields.at[pl.ds(group, couples)], obs_fields.at[pl.ds(group + couples, couples)]),
        oh_send, oh_recv,
    )
    for c in range(group):
        obs_fields[c, :, pl.ds(full, LANES)] = jnp.zeros((rows, LANES), jnp.float32)
        obs_fields[c, :, pl.ds(0, width)] = obs_ref[c]
    for p in range(couples):
        one, two = obs_fields[p], obs_fields[p + couples]
        obs_halo[0, p] = jnp.where(upper(padded), one, turn(two))
        obs_halo[1, p] = jnp.where(upper(padded), turn(one), two)
    start_both(obs_copies)
    recv_both(obs_copies)
    values = obs_fields[...].reshape(2 * group * rows, padded)
    obs_sm[...] = split_dot(obs_band_ref[...], values, 3).reshape(2 * group, rows, padded)
    lon_blur(obs_sm, group, width)

    def take_fields(k):
        f_own(k).wait()
        for h in range(len(ranges)):
            for shift in range(1, ens_n):
                f_main(k, h, shift).wait_recv()

            if h == last:
                def unpack(source, carry):
                    tile = rests[source, k]
                    for m in range(local):
                        fields[k, source * local + m, :, pl.ds(full, LANES)] = (
                            pltpu.roll(tile, LANES - m * rest, 1) if m else tile
                        )
                    return carry

                lax.fori_loop(0, ens_n, unpack, 0, unroll=True)

            def pack_halo(p, carry):
                one, two = fields[k, p, :, lanes(h)], fields[k, p + pairs, :, lanes(h)]
                mask = upper(one.shape[1])
                halo_out[k, 0, p, :, lanes(h)] = jnp.where(mask, one, turn(two))
                halo_out[k, 1, p, :, lanes(h)] = jnp.where(mask, turn(one), two)
                return carry

            lax.fori_loop(0, pairs, pack_halo, 0, unroll=4 if pairs % 4 == 0 else 1)
            start_both(halo_copies(k, h))

        @pl.when(k + 1 < group)
        def _():
            start_main(k + 1)

    def forward(k):
        def smooth_block(b, carry):
            at = pl.ds(pl.multiple_of(b * block, block), block)
            values = fields[k, :, :, at].reshape(total_rows, block)
            smooth[:, :, at] = split_dot(band_ref[...], values, 3).reshape(2 * members, rows, block)
            return carry

        for h, (low, high) in enumerate(ranges):
            recv_both(halo_copies(k, h))
            lax.fori_loop(low // block, high // block, smooth_block, 0, unroll=True)
        lon_blur(smooth, members, width)

    def interact(k):
        weight = factor_ref[me * group + k] * jnp.broadcast_to(weight_ref[:, :1], (rows, LANES))
        pull = 0.95 / (members - 1)
        tiles = padded // LANES

        def couple(i, carry):
            scale, t = i // tiles, i % tiles
            at = pl.ds(pl.multiple_of(t * LANES, LANES), LANES)
            base = scale * members
            held = [smooth[base + m, :, at] for m in range(members)]
            sums = [None] * members
            for m in range(members):
                for other in range(m):
                    force = slope(held[m] - held[other])
                    sums[m] = force if sums[m] is None else sums[m] + force
                    sums[other] = -force if sums[other] is None else sums[other] - force
            analysis = obs_sm[scale * group + k, :, at]
            for m in range(members):
                smooth[base + m, :, at] = weight * (slope(held[m] - analysis) - pull * sums[m])
            return carry

        lax.fori_loop(0, 2 * tiles, couple, 0)

    def backward(k):
        lon_blur(smooth, members, width)

        def back_block(b, carry):
            at = pl.ds(pl.multiple_of(b * block, block), block)
            values = smooth[:, :, at].reshape(total_rows, block)
            out = split_dot(back_ref[...], values, 2).reshape(2 * members, rows, block)
            result[k, :, :, at] = out[:members]
            edge_out[k, 0, :, :, at] = out[members : members + pairs]
            edge_out[k, 1, :, :, at] = out[members + pairs :]
            return carry

        for h, (low, high) in enumerate(ranges):
            lax.fori_loop(low // block, high // block, back_block, 0, unroll=True)
            start_both(edge_copies(k, h))

    def b_main(k, h, shift):
        target = peer(shift)
        return pltpu.make_async_remote_copy(
            src_ref=result.at[k, pl.ds(target * local, local), :, sent_lanes(h)],
            dst_ref=main_ref.at[:, me * group + k, :, sent_lanes(h)],
            send_sem=b_send.at[k, h, shift], recv_sem=b_recv.at[k, h, shift],
            device_id={"ens": target}, device_id_type=MESH,
        )

    def b_rest(shift):
        target = peer(shift)
        return pltpu.make_async_remote_copy(
            src_ref=result_rest.at[target], dst_ref=rest_ref.at[pl.ds(me * group, group)],
            send_sem=br_send.at[shift], recv_sem=br_recv.at[shift],
            device_id={"ens": target}, device_id_type=MESH,
        )

    def b_own(k):
        return pltpu.make_async_copy(
            result.at[k, pl.ds(me * local, local), :, pl.ds(0, full)],
            main_ref.at[:, me * group + k, :, pl.ds(0, full)], bown_sem.at[k],
        )

    def write(k, source):
        channel = source * group + k
        return pltpu.make_async_copy(
            main_ref.at[:, channel], out_ref.at[:, channel], out_sem.at[k, source]
        )

    def finish(k):
        for h in range(len(ranges)):
            recv_both(edge_copies(k, h))

            def add(p, carry):
                low, high = edge_in[k, 0, p, :, lanes(h)], edge_in[k, 1, p, :, lanes(h)]
                mask = upper(low.shape[1])
                one, two = result[k, p, :, lanes(h)], result[k, p + pairs, :, lanes(h)]
                result[k, p, :, lanes(h)] = one + jnp.where(mask, low, turn(high))
                result[k, p + pairs, :, lanes(h)] = two + jnp.where(mask, turn(low), high)
                return carry

            lax.fori_loop(0, pairs, add, 0, unroll=4 if pairs % 4 == 0 else 1)
            for shift in range(1, ens_n):
                b_main(k, h, shift).start()

        def pack(target, carry):
            result_rest[target, k] = packed(
                [result[k, target * local + m, :, pl.ds(full, LANES)] for m in range(local)]
            )
            return carry

        lax.fori_loop(0, ens_n, pack, 0, unroll=True)
        b_own(k).start()

    for shift in range(1, ens_n):
        f_rest(shift).wait_recv()
    take_fields(0)

    def turn_of(k, carry):
        forward(k)

        @pl.when(k + 1 < group)
        def _():
            take_fields(k + 1)

        interact(k)

        backward(k)

        @pl.when(k > 0)
        def _():
            finish(k - 1)


        return carry

    lax.fori_loop(0, group, turn_of, 0)
    finish(group - 1)
    for shift in range(1, ens_n):
        b_rest(shift).start()
    rest_ref[pl.ds(me * group, group)] = result_rest[me]

    sent_both(obs_copies)

    def drain(k, carry):
        for h in range(len(ranges)):
            for shift in range(1, ens_n):
                f_main(k, h, shift).wait_send()
            sent_both(halo_copies(k, h))
            sent_both(edge_copies(k, h))
        return carry

    lax.fori_loop(0, group, drain, 0)
    for shift in range(1, ens_n):
        f_rest(shift).wait_send()
        b_rest(shift).wait()

    def collect(k, carry):
        for h in range(len(ranges)):
            for shift in range(1, ens_n):
                b_main(k, h, shift).wait()
        b_own(k).wait()

        def unpack(source, inner):
            channel = source * group + k
            tile = rest_ref[channel]
            for m in range(local):
                main_ref[m, channel, :, pl.ds(full, rest)] = tile[:, m * rest : (m + 1) * rest]
            write(k, source).start()
            return inner

        lax.fori_loop(0, ens_n, unpack, 0, unroll=True)
        return carry

    lax.fori_loop(0, group, collect, 0)

    def close(k, carry):
        for source in range(ens_n):
            write(k, source).wait()
        return carry

    lax.fori_loop(0, group, close, 0)


def pass_on(in_ref, out_ref, held, in_sem, out_sem):
    local, channels = in_ref.shape[:2]
    size = channels // COPIES
    parts = [(m, pl.ds(part * size, size)) for m in range(local) for part in range(COPIES)]
    reads = [pltpu.make_async_copy(in_ref.at[at], held.at[at], in_sem.at[i]) for i, at in enumerate(parts)]
    writes = [pltpu.make_async_copy(held.at[at], out_ref.at[at], out_sem.at[i]) for i, at in enumerate(parts)]
    for read in reads:
        read.start()
    for read, write in zip(reads, writes):
        read.wait()
        write.start()
    for write in writes:
        write.wait()


def body(prediction_array, verifying_analysis, variable_penalty_factor):
    local, channels, rows, width = prediction_array.shape
    group = verifying_analysis.shape[0]
    ens_n, lat_n = lax.axis_size("ens"), lax.axis_size("lat")
    members = local * ens_n
    pairs = members // 2
    full = width // LANES * LANES
    rest = width - full
    padded = full + LANES
    assert rows % 8 == 0 and rows // 2 >= COARSE and local * rest <= LANES and channels == group * ens_n
    assert members % 2 == 0 and group % 2 == 0 and LANES - rest >= 4 * COARSE

    bands = band_matrices(members, rows)
    band = jnp.asarray(bands, jnp.bfloat16)
    back = jnp.asarray(bands.transpose(0, 2, 1), jnp.bfloat16)
    square = bands.shape[1]
    obs_bands = band_matrices(group, rows)
    obs_band = jnp.asarray(np.concatenate([obs_bands] * 3, axis=2), jnp.bfloat16)
    ids = np.arange(lat_n * rows).astype(np.float32)
    degrees = np.float32(0.25) * (ids - np.float32((lat_n * rows - 1) / 2.0))
    weights = np.cos(degrees * np.float32(np.pi / 180.0)).astype(np.float32).reshape(lat_n, rows, 1)
    weights = jnp.asarray(np.pad(weights, ((0, 0), (0, 0), (0, LANES - 1))))

    dims = (ens_n, lat_n, local, members, group, rows, width)
    hbm = pl.BlockSpec(memory_space=pltpu.HBM)
    f32 = jnp.float32
    dma = pltpu.SemaphoreType.DMA
    cells = group * padded * rows
    gathered = pl.pallas_call(
        functools.partial(kernel, dims),
        out_shape=jax.ShapeDtypeStruct((local, channels, rows, width), f32),
        in_specs=[hbm, hbm, pl.BlockSpec(memory_space=pltpu.SMEM), hbm, hbm, hbm, hbm],
        out_specs=pl.BlockSpec(memory_space=pl.ANY),
        scratch_shapes=[
            pltpu.VMEM((local, channels, rows, width), f32),
            pltpu.VMEM((channels, rows, LANES), f32),
            pltpu.VMEM(verifying_analysis.shape, f32),
            pltpu.VMEM(weights.shape[1:], f32),
            pltpu.VMEM((square, 3 * square), jnp.bfloat16),
            pltpu.VMEM((square, 2 * square), jnp.bfloat16),
            pltpu.VMEM(obs_band.shape[1:], jnp.bfloat16),
            pltpu.VMEM((local, channels, rows, width), f32),
            pltpu.VMEM((group, members + 2 * pairs, rows, padded), f32),
            pltpu.VMEM((ens_n, group, rows, LANES), f32),
            pltpu.VMEM((ens_n, group, rows, LANES), f32),
            pltpu.VMEM((group, 2, pairs, rows, padded), f32),
            pltpu.VMEM((2 * group, rows, padded), f32),
            pltpu.VMEM((2, group // 2, rows, padded), f32),
            pltpu.VMEM((2 * group, rows, padded), f32),
            pltpu.VMEM((2 * members, rows, padded), f32),
            pltpu.VMEM((group, members, rows, padded), f32),
            pltpu.VMEM((ens_n, group, rows, LANES), f32),
            pltpu.VMEM((group, 2, pairs, rows, padded), f32),
            pltpu.VMEM((group, 2, pairs, rows, padded), f32),
            dma((group, 2, ens_n)), dma((group, 2, ens_n)), dma((ens_n,)), dma((ens_n,)),
            dma((group,)), dma,
            dma((group, 2, 2)), dma((group, 2, 2)), dma((2,)), dma((2,)), dma((group, 2, 2)), dma((group, 2, 2)),
            dma((group, 2, ens_n)), dma((group, 2, ens_n)), dma((ens_n,)), dma((ens_n,)),
            dma((group,)), dma((8,)), dma((group, ens_n)),
        ],
        compiler_params=pltpu.CompilerParams(
            collective_id=0, has_side_effects=True, vmem_limit_bytes=GRANT
        ),
        cost_estimate=pl.CostEstimate(
            flops=cells * members * members * 6, bytes_accessed=cells * members * 8,
            transcendentals=cells * members * members,
        ),
    )(prediction_array, verifying_analysis, variable_penalty_factor, weights, band, back, obs_band)
    return pl.pallas_call(
        pass_on,
        out_shape=jax.ShapeDtypeStruct(gathered.shape, f32),
        in_specs=[hbm],
        out_specs=hbm,
        scratch_shapes=[pltpu.VMEM(gathered.shape, f32), dma((local * COPIES,)), dma((local * COPIES,))],
        compiler_params=pltpu.CompilerParams(vmem_limit_bytes=GRANT),
    )(gathered)


def solution(mesh):
    placed = (P("ens", None, "lat", None), P("ens", "lat", None), P())
    return jax.shard_map(
        body, mesh=mesh, in_specs=placed, out_specs=P("ens", None, "lat", None), check_vma=False
    )
```

```python
import functools
import math

import jax
import jax.numpy as jnp
import numpy as np
from jax import lax
from jax.experimental import pallas as pl
from jax.experimental.pallas import tpu as pltpu
from jax.sharding import PartitionSpec as P

COARSE = 3
LANES = 128
COPIES = 4
GRANT = 62 * 1024 * 1024
MESH = pl.DeviceIdType.MESH


def round_up(value, unit):
    return -(-value // unit) * unit


def band_matrices(fields, rows):
    half = rows // 2
    pairs = fields // 2
    out = np.zeros((4, 2 * fields * rows, 2 * fields * rows), np.float32)
    window = 2 * rows
    band = 0.5 * np.eye(window) + 0.25 * np.eye(window, k=1) + 0.25 * np.eye(window, k=-1)
    places = np.arange(window) - half
    for variant in range(4):
        keep = np.ones(window)
        if variant & 1:
            keep[places < 0] = 0.0
        if variant & 2:
            keep[places >= rows] = 0.0
        step = keep[:, None] * band * keep[None, :]
        scales = (step, np.linalg.matrix_power(step, COARSE))
        for scale, matrix in enumerate(scales):
            matrix = matrix[half : half + rows]
            for field in range(fields):
                at = (scale * fields + field) * rows
                out[variant, at : at + rows, field * rows : (field + 1) * rows] = matrix[:, half : half + rows]
                tile, part = field % pairs, field // pairs
                low = (fields + tile) * rows + part * half
                out[variant, at : at + rows, low : low + half] = matrix[:, :half]
                high = (fields + pairs + tile) * rows + part * half
                out[variant, at : at + rows, high : high + half] = matrix[:, half + rows :]
    return out


def split_dot(matrix, values, parts):
    pieces = []
    for _ in range(parts):
        piece = values.astype(jnp.bfloat16)
        pieces.append(piece)
        values = values - piece.astype(jnp.float32)
    return jnp.dot(matrix, jnp.concatenate(pieces, axis=0), preferred_element_type=jnp.float32)


def wrapped(tiles, width):
    whole = width // LANES
    rest = width - whole * LANES
    last = tiles[:, whole * LANES :]
    lane = lax.broadcasted_iota(jnp.int32, last.shape, 1)
    ahead = pltpu.roll(tiles[:, :LANES], rest, 1)
    behind = pltpu.roll(last, LANES - rest, 1)
    last = jnp.where(lane < rest, last, jnp.where(lane < (LANES + rest) // 2, ahead, behind))
    return jnp.concatenate([tiles[:, : whole * LANES], last], axis=1)


def lon_pass(tiles, passes):
    size = tiles.shape[1]
    total = math.comb(2 * passes, passes) / 4.0**passes * tiles
    for far in range(1, passes + 1):
        both = pltpu.roll(tiles, far, 1) + pltpu.roll(tiles, size - far, 1)
        total = total + math.comb(2 * passes, passes + far) / 4.0**passes * both
    return total


def lon_blur(ref, count, width):
    def step(field, carry):
        ref[field] = lon_pass(wrapped(ref[field], width), 1)
        ref[count + field] = lon_pass(wrapped(ref[count + field], width), COARSE)
        return carry

    lax.fori_loop(0, count, step, 0, unroll=4 if count % 4 == 0 else 2)


def slope(differ):
    return differ * lax.rsqrt(differ * differ + 0.01)


def kernel(
    dims,
    in_ref, obs_hbm, factor_ref, weight_hbm, band_hbm, back_hbm, obs_band_hbm,
    out_ref,
    main_ref, rest_ref, obs_ref, weight_ref, band_ref, back_ref, obs_band_ref,
    staged, fields, rests, rest_out, halo_out, obs_fields, obs_halo, obs_sm, smooth, result, result_rest,
    edge_out, edge_in,
    f_send, f_recv, fr_send, fr_recv, own_sem, stage_sem,
    h_send, h_recv, oh_send, oh_recv, e_send, e_recv,
    b_send, b_recv, br_send, br_recv, bown_sem, load_sem, out_sem,
):
    ens_n, lat_n, local, members, group, rows, width = dims
    half = rows // 2
    pairs = members // 2
    full = width // LANES * LANES
    rest = width - full
    padded = full + LANES
    total_rows = 2 * members * rows
    block = 2 * LANES if padded % (2 * LANES) == 0 else LANES
    cut = (padded // block + 1) // 2 * block
    ranges = ((0, cut), (cut, padded))
    last = len(ranges) - 1
    me = lax.axis_index("ens")
    lat = lax.axis_index("lat")
    has_low = lat > 0
    has_high = lat < lat_n - 1
    variant = (lat == 0).astype(jnp.int32) + 2 * (lat == lat_n - 1).astype(jnp.int32)

    def peer(shift):
        return lax.rem(me + shift, ens_n)

    barrier = pltpu.get_barrier_semaphore()
    for shift in range(1, ens_n):
        pl.semaphore_signal(barrier, inc=1, device_id={"ens": peer(shift)}, device_id_type=MESH)

    @pl.when(has_low)
    def _():
        pl.semaphore_signal(barrier, inc=1, device_id={"lat": lat - 1}, device_id_type=MESH)

    @pl.when(has_high)
    def _():
        pl.semaphore_signal(barrier, inc=1, device_id={"lat": lat + 1}, device_id_type=MESH)

    stage = pltpu.make_async_copy(in_ref, staged, stage_sem)
    stage.start()
    loads = [
        pltpu.make_async_copy(source, target, load_sem.at[i])
        for i, (source, target) in enumerate((
            (obs_hbm, obs_ref),
            (weight_hbm.at[lat], weight_ref),
            *((band_hbm.at[variant], band_ref.at[:, pl.ds(part * total_rows, total_rows)]) for part in range(3)),
            *((back_hbm.at[variant], back_ref.at[:, pl.ds(part * total_rows, total_rows)]) for part in range(2)),
            (obs_band_hbm.at[variant], obs_band_ref),
        ))
    ]
    for load in loads:
        load.start()

    def zero_edges(low):
        at = members if low else members + pairs
        side = 0 if low else 1

        def clear(k, carry):
            def tile(p, inner):
                fields[k, at + p] = jnp.zeros((rows, padded), jnp.float32)
                edge_in[k, side, p] = jnp.zeros((rows, padded), jnp.float32)
                return inner

            lax.fori_loop(0, pairs, tile, 0)
            return carry

        lax.fori_loop(0, group, clear, 0)
        obs_at = group if low else group + group // 2
        for p in range(group // 2):
            obs_fields[obs_at + p] = jnp.zeros((rows, padded), jnp.float32)

    pl.semaphore_wait(barrier, ens_n - 1 + has_low.astype(jnp.int32) + has_high.astype(jnp.int32))

    def sent_lanes(h):
        low, high = ranges[h]
        return pl.ds(low, min(high, full) - low)

    def f_main(k, h, shift):
        target = peer(shift)
        return pltpu.make_async_remote_copy(
            src_ref=in_ref.at[:, target * group + k, :, sent_lanes(h)],
            dst_ref=fields.at[k, pl.ds(me * local, local), :, sent_lanes(h)],
            send_sem=f_send.at[k, h, shift], recv_sem=f_recv.at[k, h, shift],
            device_id={"ens": target}, device_id_type=MESH,
        )

    def f_rest(shift):
        target = peer(shift)
        return pltpu.make_async_remote_copy(
            src_ref=rest_out.at[target], dst_ref=rests.at[me],
            send_sem=fr_send.at[shift], recv_sem=fr_recv.at[shift],
            device_id={"ens": target}, device_id_type=MESH,
        )

    def f_own(k):
        return pltpu.make_async_copy(
            in_ref.at[:, me * group + k, :, pl.ds(0, full)],
            fields.at[k, pl.ds(me * local, local), :, pl.ds(0, full)],
            own_sem.at[k],
        )

    def start_main(k):
        for h in range(len(ranges)):
            for shift in range(1, ens_n):
                f_main(k, h, shift).start()
        f_own(k).start()

    lane = lax.broadcasted_iota(jnp.int32, (rows, LANES), 1)

    def packed(tiles):
        total = tiles[0]
        for m in range(1, local):
            total = jnp.where(lane < m * rest, total, pltpu.roll(tiles[m], m * rest, 1))
        return total

    def pack_rest(target, carry):
        for k in range(group):
            rest_out[target, k] = packed([
                jnp.concatenate(
                    [staged[m, target * group + k, :, pl.ds(full, rest)],
                     jnp.zeros((rows, LANES - rest), jnp.float32)], axis=1)
                for m in range(local)
            ])
        return carry

    start_main(0)

    @pl.when(jnp.logical_not(has_low))
    def _():
        zero_edges(True)

    @pl.when(jnp.logical_not(has_high))
    def _():
        zero_edges(False)

    stage.wait()
    lax.fori_loop(0, ens_n, pack_rest, 0)
    rests[me] = rest_out[me]
    for shift in range(1, ens_n):
        f_rest(shift).start()

    def upper(size):
        return lax.broadcasted_iota(jnp.int32, (rows, size), 0) < half

    def turn(tile):
        return pltpu.roll(tile, half, 0)

    def neighbour_copies(source, targets, send, recv):
        return (
            pltpu.make_async_remote_copy(
                src_ref=source[0], dst_ref=targets[1], send_sem=send.at[0], recv_sem=recv.at[1],
                device_id={"lat": lat - 1}, device_id_type=MESH,
            ),
            pltpu.make_async_remote_copy(
                src_ref=source[1], dst_ref=targets[0], send_sem=send.at[1], recv_sem=recv.at[0],
                device_id={"lat": lat + 1}, device_id_type=MESH,
            ),
        )

    def start_both(copies):
        @pl.when(has_low)
        def _():
            copies[0].start()

        @pl.when(has_high)
        def _():
            copies[1].start()

    def recv_both(copies):
        @pl.when(has_low)
        def _():
            copies[1].wait_recv()

        @pl.when(has_high)
        def _():
            copies[0].wait_recv()

    def sent_both(copies):
        @pl.when(has_low)
        def _():
            copies[0].wait_send()

        @pl.when(has_high)
        def _():
            copies[1].wait_send()

    def lanes(h):
        return pl.ds(ranges[h][0], ranges[h][1] - ranges[h][0])

    def halo_copies(k, h):
        return neighbour_copies(
            (halo_out.at[k, 0, :, :, lanes(h)], halo_out.at[k, 1, :, :, lanes(h)]),
            (fields.at[k, pl.ds(members, pairs), :, lanes(h)],
             fields.at[k, pl.ds(members + pairs, pairs), :, lanes(h)]),
            h_send.at[k, h], h_recv.at[k, h],
        )

    def edge_copies(k, h):
        return neighbour_copies(
            (edge_out.at[k, 0, :, :, lanes(h)], edge_out.at[k, 1, :, :, lanes(h)]),
            (edge_in.at[k, 0, :, :, lanes(h)], edge_in.at[k, 1, :, :, lanes(h)]),
            e_send.at[k, h], e_recv.at[k, h],
        )

    for load in loads:
        load.wait()
    couples = group // 2
    obs_copies = neighbour_copies(
        (obs_halo.at[0], obs_halo.at[1]),
        (obs_fields.at[pl.ds(group, couples)], obs_fields.at[pl.ds(group + couples, couples)]),
        oh_send, oh_recv,
    )
    for c in range(group):
        obs_fields[c, :, pl.ds(full, LANES)] = jnp.zeros((rows, LANES), jnp.float32)
        obs_fields[c, :, pl.ds(0, width)] = obs_ref[c]
    for p in range(couples):
        one, two = obs_fields[p], obs_fields[p + couples]
        obs_halo[0, p] = jnp.where(upper(padded), one, turn(two))
        obs_halo[1, p] = jnp.where(upper(padded), turn(one), two)
    start_both(obs_copies)
    recv_both(obs_copies)
    values = obs_fields[...].reshape(2 * group * rows, padded)
    obs_sm[...] = split_dot(obs_band_ref[...], values, 3).reshape(2 * group, rows, padded)
    lon_blur(obs_sm, group, width)

    def take_fields(k):
        f_own(k).wait()
        for h in range(len(ranges)):
            for shift in range(1, ens_n):
                f_main(k, h, shift).wait_recv()

            if h == last:
                def unpack(source, carry):
                    tile = rests[source, k]
                    for m in range(local):
                        fields[k, source * local + m, :, pl.ds(full, LANES)] = (
                            pltpu.roll(tile, LANES - m * rest, 1) if m else tile
                        )
                    return carry

                lax.fori_loop(0, ens_n, unpack, 0, unroll=True)

            def pack_halo(p, carry):
                one, two = fields[k, p, :, lanes(h)], fields[k, p + pairs, :, lanes(h)]
                mask = upper(one.shape[1])
                halo_out[k, 0, p, :, lanes(h)] = jnp.where(mask, one, turn(two))
                halo_out[k, 1, p, :, lanes(h)] = jnp.where(mask, turn(one), two)
                return carry

            lax.fori_loop(0, pairs, pack_halo, 0, unroll=4 if pairs % 4 == 0 else 1)
            start_both(halo_copies(k, h))

        @pl.when(k + 1 < group)
        def _():
            start_main(k + 1)

    def forward(k):
        def smooth_block(b, carry):
            at = pl.ds(pl.multiple_of(b * block, block), block)
            values = fields[k, :, :, at].reshape(total_rows, block)
            smooth[:, :, at] = split_dot(band_ref[...], values, 3).reshape(2 * members, rows, block)
            return carry

        for h, (low, high) in enumerate(ranges):
            recv_both(halo_copies(k, h))
            lax.fori_loop(low // block, high // block, smooth_block, 0, unroll=True)
        lon_blur(smooth, members, width)

    def interact(k):
        weight = factor_ref[me * group + k] * jnp.broadcast_to(weight_ref[:, :1], (rows, LANES))
        pull = 0.95 / (members - 1)
        tiles = padded // LANES

        def couple(i, carry):
            scale, t = i // tiles, i % tiles
            at = pl.ds(pl.multiple_of(t * LANES, LANES), LANES)
            base = scale * members
            held = [smooth[base + m, :, at] for m in range(members)]
            sums = [None] * members
            for m in range(members):
                for other in range(m):
                    force = slope(held[m] - held[other])
                    sums[m] = force if sums[m] is None else sums[m] + force
                    sums[other] = -force if sums[other] is None else sums[other] - force
            analysis = obs_sm[scale * group + k, :, at]
            for m in range(members):
                smooth[base + m, :, at] = weight * (slope(held[m] - analysis) - pull * sums[m])
            return carry

        lax.fori_loop(0, 2 * tiles, couple, 0, unroll=2)

    def backward(k):
        lon_blur(smooth, members, width)

        def back_block(b, carry):
            at = pl.ds(pl.multiple_of(b * block, block), block)
            values = smooth[:, :, at].reshape(total_rows, block)
            out = split_dot(back_ref[...], values, 2).reshape(2 * members, rows, block)
            result[k, :, :, at] = out[:members]
            edge_out[k, 0, :, :, at] = out[members : members + pairs]
            edge_out[k, 1, :, :, at] = out[members + pairs :]
            return carry

        for h, (low, high) in enumerate(ranges):
            lax.fori_loop(low // block, high // block, back_block, 0, unroll=True)
            start_both(edge_copies(k, h))

    def b_main(k, h, shift):
        target = peer(shift)
        return pltpu.make_async_remote_copy(
            src_ref=result.at[k, pl.ds(target * local, local), :, sent_lanes(h)],
            dst_ref=main_ref.at[:, me * group + k, :, sent_lanes(h)],
            send_sem=b_send.at[k, h, shift], recv_sem=b_recv.at[k, h, shift],
            device_id={"ens": target}, device_id_type=MESH,
        )

    def b_rest(shift):
        target = peer(shift)
        return pltpu.make_async_remote_copy(
            src_ref=result_rest.at[target], dst_ref=rest_ref.at[pl.ds(me * group, group)],
            send_sem=br_send.at[shift], recv_sem=br_recv.at[shift],
            device_id={"ens": target}, device_id_type=MESH,
        )

    def b_own(k):
        return pltpu.make_async_copy(
            result.at[k, pl.ds(me * local, local), :, pl.ds(0, full)],
            main_ref.at[:, me * group + k, :, pl.ds(0, full)], bown_sem.at[k],
        )

    def write(k, source):
        channel = source * group + k
        return pltpu.make_async_copy(
            main_ref.at[:, channel], out_ref.at[:, channel], out_sem.at[k, source]
        )

    def finish(k):
        for h in range(len(ranges)):
            recv_both(edge_copies(k, h))

            def add(p, carry):
                low, high = edge_in[k, 0, p, :, lanes(h)], edge_in[k, 1, p, :, lanes(h)]
                mask = upper(low.shape[1])
                one, two = result[k, p, :, lanes(h)], result[k, p + pairs, :, lanes(h)]
                result[k, p, :, lanes(h)] = one + jnp.where(mask, low, turn(high))
                result[k, p + pairs, :, lanes(h)] = two + jnp.where(mask, turn(low), high)
                return carry

            lax.fori_loop(0, pairs, add, 0, unroll=4 if pairs % 4 == 0 else 1)
            for shift in range(1, ens_n):
                b_main(k, h, shift).start()

        def pack(target, carry):
            result_rest[target, k] = packed(
                [result[k, target * local + m, :, pl.ds(full, LANES)] for m in range(local)]
            )
            return carry

        lax.fori_loop(0, ens_n, pack, 0, unroll=True)
        b_own(k).start()

    for shift in range(1, ens_n):
        f_rest(shift).wait_recv()
    take_fields(0)

    def turn_of(k, carry):
        forward(k)

        @pl.when(k + 1 < group)
        def _():
            take_fields(k + 1)

        interact(k)

        @pl.when(k > 0)
        def _():
            finish(k - 1)

        backward(k)

        return carry

    lax.fori_loop(0, group, turn_of, 0)
    finish(group - 1)
    for shift in range(1, ens_n):
        b_rest(shift).start()
    rest_ref[pl.ds(me * group, group)] = result_rest[me]

    sent_both(obs_copies)

    def drain(k, carry):
        for h in range(len(ranges)):
            for shift in range(1, ens_n):
                f_main(k, h, shift).wait_send()
            sent_both(halo_copies(k, h))
            sent_both(edge_copies(k, h))
        return carry

    lax.fori_loop(0, group, drain, 0)
    for shift in range(1, ens_n):
        f_rest(shift).wait_send()
        b_rest(shift).wait()

    def collect(k, carry):
        for h in range(len(ranges)):
            for shift in range(1, ens_n):
                b_main(k, h, shift).wait()
        b_own(k).wait()

        def unpack(source, inner):
            channel = source * group + k
            tile = rest_ref[channel]
            for m in range(local):
                main_ref[m, channel, :, pl.ds(full, rest)] = tile[:, m * rest : (m + 1) * rest]
            write(k, source).start()
            return inner

        lax.fori_loop(0, ens_n, unpack, 0, unroll=True)
        return carry

    lax.fori_loop(0, group, collect, 0)

    def close(k, carry):
        for source in range(ens_n):
            write(k, source).wait()
        return carry

    lax.fori_loop(0, group, close, 0)


def pass_on(in_ref, out_ref, held, in_sem, out_sem):
    local, channels = in_ref.shape[:2]
    size = channels // COPIES
    parts = [(m, pl.ds(part * size, size)) for m in range(local) for part in range(COPIES)]
    reads = [pltpu.make_async_copy(in_ref.at[at], held.at[at], in_sem.at[i]) for i, at in enumerate(parts)]
    writes = [pltpu.make_async_copy(held.at[at], out_ref.at[at], out_sem.at[i]) for i, at in enumerate(parts)]
    for read in reads:
        read.start()
    for read, write in zip(reads, writes):
        read.wait()
        write.start()
    for write in writes:
        write.wait()


def body(prediction_array, verifying_analysis, variable_penalty_factor):
    local, channels, rows, width = prediction_array.shape
    group = verifying_analysis.shape[0]
    ens_n, lat_n = lax.axis_size("ens"), lax.axis_size("lat")
    members = local * ens_n
    pairs = members // 2
    full = width // LANES * LANES
    rest = width - full
    padded = full + LANES
    assert rows % 8 == 0 and rows // 2 >= COARSE and local * rest <= LANES and channels == group * ens_n
    assert members % 2 == 0 and group % 2 == 0 and LANES - rest >= 4 * COARSE

    bands = band_matrices(members, rows)
    band = jnp.asarray(bands, jnp.bfloat16)
    back = jnp.asarray(bands.transpose(0, 2, 1), jnp.bfloat16)
    square = bands.shape[1]
    obs_bands = band_matrices(group, rows)
    obs_band = jnp.asarray(np.concatenate([obs_bands] * 3, axis=2), jnp.bfloat16)
    ids = np.arange(lat_n * rows).astype(np.float32)
    degrees = np.float32(0.25) * (ids - np.float32((lat_n * rows - 1) / 2.0))
    weights = np.cos(degrees * np.float32(np.pi / 180.0)).astype(np.float32).reshape(lat_n, rows, 1)
    weights = jnp.asarray(np.pad(weights, ((0, 0), (0, 0), (0, LANES - 1))))

    dims = (ens_n, lat_n, local, members, group, rows, width)
    hbm = pl.BlockSpec(memory_space=pltpu.HBM)
    f32 = jnp.float32
    dma = pltpu.SemaphoreType.DMA
    cells = group * padded * rows
    gathered = pl.pallas_call(
        functools.partial(kernel, dims),
        out_shape=jax.ShapeDtypeStruct((local, channels, rows, width), f32),
        in_specs=[hbm, hbm, pl.BlockSpec(memory_space=pltpu.SMEM), hbm, hbm, hbm, hbm],
        out_specs=pl.BlockSpec(memory_space=pl.ANY),
        scratch_shapes=[
            pltpu.VMEM((local, channels, rows, width), f32),
            pltpu.VMEM((channels, rows, LANES), f32),
            pltpu.VMEM(verifying_analysis.shape, f32),
            pltpu.VMEM(weights.shape[1:], f32),
            pltpu.VMEM((square, 3 * square), jnp.bfloat16),
            pltpu.VMEM((square, 2 * square), jnp.bfloat16),
            pltpu.VMEM(obs_band.shape[1:], jnp.bfloat16),
            pltpu.VMEM((local, channels, rows, width), f32),
            pltpu.VMEM((group, members + 2 * pairs, rows, padded), f32),
            pltpu.VMEM((ens_n, group, rows, LANES), f32),
            pltpu.VMEM((ens_n, group, rows, LANES), f32),
            pltpu.VMEM((group, 2, pairs, rows, padded), f32),
            pltpu.VMEM((2 * group, rows, padded), f32),
            pltpu.VMEM((2, group // 2, rows, padded), f32),
            pltpu.VMEM((2 * group, rows, padded), f32),
            pltpu.VMEM((2 * members, rows, padded), f32),
            pltpu.VMEM((group, members, rows, padded), f32),
            pltpu.VMEM((ens_n, group, rows, LANES), f32),
            pltpu.VMEM((group, 2, pairs, rows, padded), f32),
            pltpu.VMEM((group, 2, pairs, rows, padded), f32),
            dma((group, 2, ens_n)), dma((group, 2, ens_n)), dma((ens_n,)), dma((ens_n,)),
            dma((group,)), dma,
            dma((group, 2, 2)), dma((group, 2, 2)), dma((2,)), dma((2,)), dma((group, 2, 2)), dma((group, 2, 2)),
            dma((group, 2, ens_n)), dma((group, 2, ens_n)), dma((ens_n,)), dma((ens_n,)),
            dma((group,)), dma((8,)), dma((group, ens_n)),
        ],
        compiler_params=pltpu.CompilerParams(
            collective_id=0, has_side_effects=True, vmem_limit_bytes=GRANT
        ),
        cost_estimate=pl.CostEstimate(
            flops=cells * members * members * 6, bytes_accessed=cells * members * 8,
            transcendentals=cells * members * members,
        ),
    )(prediction_array, verifying_analysis, variable_penalty_factor, weights, band, back, obs_band)
    return pl.pallas_call(
        pass_on,
        out_shape=jax.ShapeDtypeStruct(gathered.shape, f32),
        in_specs=[hbm],
        out_specs=hbm,
        scratch_shapes=[pltpu.VMEM(gathered.shape, f32), dma((local * COPIES,)), dma((local * COPIES,))],
        compiler_params=pltpu.CompilerParams(vmem_limit_bytes=GRANT),
    )(gathered)


def solution(mesh):
    placed = (P("ens", None, "lat", None), P("ens", "lat", None), P())
    return jax.shard_map(
        body, mesh=mesh, in_specs=placed, out_specs=P("ens", None, "lat", None), check_vma=False
    )
```
